32 devices in a mesh: beam: 4 (over z), tile: 8 (over y, x, core).
Axes of the slice: x: 2, y: 2, z: 4, core: 2. Of those that a mesh axis runs over, the one named last changes fastest.
Arguments:
- scattering: float32 [16, 2, 1024, 256], P('beam', None, 'tile'), may hold values from -4 to 4
- potential: float32 [1024, 256], P('tile'), may hold values from -6 to 6
- row_offset: int32 [4, 8], P(None, 'tile'), may hold values from 0 to 64
- col_offset: int32 [4, 8], P(None, 'tile'), may hold values from 0 to 128
- table_index: int32 [4, 8], P(None, 'tile'), may hold values from 0 to 3
- beam_tilt: int32 [2, 16], P(None, 'beam'), may hold values from -8 to 8
- coef_table: float32 [2, 4, 16], P(None, None, 'beam'), may hold values from -1.5 to 1.5
- measured: float32 [4, 8, 128, 128], P(None, 'tile'), may hold values from 0 to 2
Outputs:
- residual: float32 [4, 8, 128, 128], P('beam', 'tile')
- gradient: float32 [1024, 256], P('tile')
The draws below stay inside these ranges and needn't reach their ends.
All inputs are finite; a program needn't handle non-finite values.
Results may differ from the reference program's by a relative error of at most 0.0002.
Values sent between devices are 32-bit elements; how exact they have to be, the bound alone decides.
A program may use at most 64 MiB of HBM per device.

```python
import math
import jax
import jax.numpy as jnp
from jax import lax

PATCH = 128
MARGIN = 32
ROWS = 128
COLS = 256
NTAB = 4
BEAMS = 16
P_TILE = 4
NR = 1024
N_TILE = 8


def set_ends(values, key, least, high):
    longest = values.shape.index(max(values.shape))
    spots = []
    for shift in (0, 1):
        where = [jax.random.randint(jax.random.fold_in(key, axis), (), 0, length) for axis, length in enumerate(values.shape)]
        where[longest] = (where[longest] + shift) % values.shape[longest]
        spots.append(tuple(where))
    return values.at[spots[0]].set(least).at[spots[1]].set(high)


def shard_levels(stream_key, extent, cuts, least, top_value):
    loudness, own = 1.0, jax.random.fold_in(stream_key, 6)
    for axis_at, blocks in cuts:
        draws = jnp.exp(jax.random.uniform(jax.random.fold_in(own, axis_at), (blocks,), jnp.float32, least / len(cuts), top_value / len(cuts)))
        loudness = loudness * jnp.repeat(draws, extent[axis_at] // blocks).reshape([-1 if axis == axis_at else 1 for axis in range(len(extent))])
    return loudness


def bell_draw(stream_key, extent, width, reach, cuts=(), held_as=jnp.bfloat16):
    result = jax.random.normal(stream_key, extent, jnp.float32) * width
    if len(cuts) > 0:
        result = shard_levels(stream_key, extent, cuts, -0.22, 0.18) * result
    return jnp.clip(result, min=-reach, max=reach).astype(held_as)


def setup_inputs(seed: int = 0) -> dict:
    keys = jax.random.split(jax.random.key(seed), 9)
    return {
        "scattering": bell_draw(keys[0], (BEAMS, 2, NR, COLS), 0.5, 4.0, ((0, 4), (2, 8)), jnp.float32),
        "potential": bell_draw(keys[1], (NR, COLS), 1.0, 6.0, ((0, 8),), jnp.float32),
        "row_offset": set_ends(jax.random.randint(keys[2], (P_TILE, N_TILE), 0, 2 * MARGIN + 1), jax.random.fold_in(keys[2], 1), 0, 2 * MARGIN).astype(jnp.int32),
        "col_offset": set_ends(jax.random.randint(keys[3], (P_TILE, N_TILE), 0, COLS - PATCH + 1), jax.random.fold_in(keys[3], 1), 0, COLS - PATCH).astype(jnp.int32),
        "table_index": set_ends(jax.random.randint(keys[4], (P_TILE, N_TILE), 0, NTAB), jax.random.fold_in(keys[4], 1), 0, NTAB - 1).astype(jnp.int32),
        "beam_tilt": set_ends(jax.random.randint(keys[5], (2, BEAMS), -8, 9), jax.random.fold_in(keys[5], 1), -8, 8).astype(jnp.int32),
        "coef_table": bell_draw(keys[6], (2, NTAB, BEAMS), BEAMS ** -0.5, 1.5, ((2, 4),), jnp.float32),
        "measured": jnp.clip(2.0 * jax.random.uniform(keys[7], (P_TILE, N_TILE, PATCH, PATCH), jnp.float32) ** shard_levels(keys[7], (P_TILE, N_TILE, PATCH, PATCH), ((1, 8),), -0.2, 0.2), 0.0, 2.0),
    }


SIGMA_SCALE = 1.0
HIGH = lax.Precision.HIGHEST

def dft_parts(inverse):
    pixel_index = jnp.arange(PATCH, dtype=jnp.int32)
    phase_turns = (pixel_index[:, None] * pixel_index[None, :] % PATCH).astype(jnp.float32)
    dft_angle = phase_turns * (2.0 * math.pi / PATCH)
    unit_scale = 1.0 / math.sqrt(PATCH)
    sin_sign = 1.0 if inverse else -1.0
    return (jnp.cos(dft_angle) * unit_scale, sin_sign * jnp.sin(dft_angle) * unit_scale)

def complex_dot(left_re, left_im, right_re, right_im):
    part_re = jnp.dot(left_re, right_re, precision=HIGH) - jnp.dot(left_im, right_im, precision=HIGH)
    part_im = jnp.dot(left_re, right_im, precision=HIGH) + jnp.dot(left_im, right_re, precision=HIGH)
    return (part_re, part_im)

def transform(value_re, value_im, table_re, table_im):
    half_re, half_im = complex_dot(table_re, table_im, value_re, value_im)
    return complex_dot(half_re, half_im, table_re, table_im)

def reference(scattering, potential, row_offset, col_offset, table_index, beam_tilt, coef_table, measured):
    wide = jnp.pad(scattering, ((0, 0), (0, 0), (MARGIN, MARGIN), (0, 0)))
    phase_map = jnp.pad(potential, ((MARGIN, MARGIN), (0, 0))) * SIGMA_SCALE
    forward_re, forward_im = dft_parts(False)
    inverse_re, inverse_im = dft_parts(True)
    tile_ids = jnp.arange(N_TILE, dtype=jnp.int32)
    start_row = (row_offset + tile_ids[None, :] * ROWS).reshape(-1).astype(jnp.int32)
    start_col = col_offset.reshape(-1).astype(jnp.int32)
    corner_row = start_row - MARGIN
    phase_turns = (beam_tilt[0][None, :] * corner_row[:, None] + beam_tilt[1][None, :] * start_col[:, None]) % PATCH
    tilt_angle = phase_turns.astype(jnp.float32) * (2.0 * math.pi / PATCH)
    picked_re = coef_table[0][table_index.reshape(-1)]
    picked_im = coef_table[1][table_index.reshape(-1)]
    coef_re = picked_re * jnp.cos(tilt_angle) + picked_im * jnp.sin(tilt_angle)
    coef_im = picked_im * jnp.cos(tilt_angle) - picked_re * jnp.sin(tilt_angle)
    observed = measured.reshape(-1, PATCH, PATCH)
    zero_index = jnp.zeros((), jnp.int32)

    def one_position(record):
        row_at, col_at, weight_re, weight_im, seen_here = record
        region = lax.dynamic_slice(wide, (zero_index, zero_index, row_at, col_at), (BEAMS, 2, PATCH, PATCH))
        wave_re = jnp.einsum('b,bij->ij', weight_re, region[:, 0], precision=HIGH) - jnp.einsum('b,bij->ij', weight_im, region[:, 1], precision=HIGH)
        wave_im = jnp.einsum('b,bij->ij', weight_re, region[:, 1], precision=HIGH) + jnp.einsum('b,bij->ij', weight_im, region[:, 0], precision=HIGH)
        local_pot = lax.dynamic_slice(phase_map, (row_at, col_at), (PATCH, PATCH))
        trans_re = jnp.cos(local_pot)
        trans_im = jnp.sin(local_pot)
        exit_re = trans_re * wave_re - trans_im * wave_im
        exit_im = trans_re * wave_im + trans_im * wave_re
        far_re, far_im = transform(exit_re, exit_im, forward_re, forward_im)
        misfit = far_re * far_re + far_im * far_im - seen_here
        back_re, back_im = transform(misfit * far_re, misfit * far_im, inverse_re, inverse_im)
        piece = SIGMA_SCALE * (exit_re * back_im - exit_im * back_re)
        return (misfit, piece)
    misfits, pieces = lax.map(one_position, (start_row, start_col, coef_re, coef_im, observed))

    def add_piece(accum_grid, record):
        row_at, col_at, piece = record
        current = lax.dynamic_slice(accum_grid, (row_at, col_at), (PATCH, PATCH))
        return (lax.dynamic_update_slice(accum_grid, current + piece, (row_at, col_at)), None)
    accum_grid, _ = lax.scan(add_piece, jnp.zeros((NR + 2 * MARGIN, COLS), jnp.float32), (start_row, start_col, pieces))
    residual = misfits.reshape(P_TILE, N_TILE, PATCH, PATCH)
    gradient = accum_grid[MARGIN:MARGIN + NR]
    return (residual, gradient)
```

```python
import functools
import math

import jax
import jax.numpy as jnp
import numpy as np
from jax import lax
from jax.experimental import pallas as pl
from jax.experimental.pallas import tpu as pltpu
from jax.sharding import PartitionSpec as P

MARGIN = 32
SIGMA_SCALE = 1.0
MESH = pl.DeviceIdType.MESH


def tables(length):
    index = np.arange(length)
    angle = (index[:, None] * index[None, :] % length) * (2.0 * math.pi / length)
    re = np.cos(angle) / math.sqrt(length)
    im = -np.sin(angle) / math.sqrt(length)
    ahead = np.block([[re, im], [-im, re]]).astype(np.float32)
    back = np.block([[re, -im], [im, re]]).astype(np.float32)
    both = np.stack([ahead, back])
    high = both.astype(jnp.bfloat16)
    low = (both - high.astype(np.float32)).astype(jnp.bfloat16)
    turns = np.arange(length) * (2.0 * math.pi / length)
    trig = np.stack([np.cos(turns), np.sin(turns)]).astype(np.float32)
    return high, low, trig


def split(value):
    high = value.astype(jnp.bfloat16)
    low = (value - high.astype(jnp.float32)).astype(jnp.bfloat16)
    return high, low


def dot(left, right):
    return jnp.dot(left, right, preferred_element_type=jnp.float32)


def split_dot(left, right):
    return dot(left[0], right[0]) + (dot(left[0], right[1]) + dot(left[1], right[0]))


def transform(stacked, left_table, right_table):
    length = stacked.shape[-1]
    half = split_dot(left_table, split(stacked))
    wide = jnp.concatenate([half[:length], half[length:]], 1)
    return split_dot(split(wide), right_table)


def kernel(
    n,
    tiles,
    row_ref,
    col_ref,
    index_ref,
    tilt_ref,
    coef_ref,
    trig_ref,
    high_ref,
    low_ref,
    scat,
    pot,
    meas,
    misfit_ref,
    grad_ref,
    loc,
    ploc,
    halo,
    phalo,
    seen,
    block,
    send_b,
    recv_a,
    recv_b,
    trans,
    piece,
    recv_p,
    strip,
    rims,
    local_sem,
    halo_send,
    halo_recv,
    a_send,
    a_recv,
    b_send,
    b_recv,
    p_send,
    p_recv,
    rim_send,
    rim_recv,
):
    me = lax.axis_index("beam")
    tile = lax.axis_index("tile")
    beams = scat.shape[0]
    rows, cols = scat.shape[2], scat.shape[3]
    patch = seen.shape[-1]
    middle = patch - 2 * MARGIN

    local = [
        pltpu.make_async_copy(scat, loc, local_sem.at[0]),
        pltpu.make_async_copy(pot, ploc, local_sem.at[1]),
        pltpu.make_async_copy(meas.at[me, 0], seen, local_sem.at[2]),
    ]
    for copy in local:
        copy.start()

    barrier = pltpu.get_barrier_semaphore()
    for k in range(1, n):
        pl.semaphore_signal(
            barrier, inc=1, device_id={"beam": lax.rem(me + k, n)}, device_id_type=MESH
        )
    has_up = tile > 0
    has_down = tile < tiles - 1

    @pl.when(has_up)
    def _():
        pl.semaphore_signal(barrier, inc=1, device_id={"tile": tile - 1}, device_id_type=MESH)

    @pl.when(has_down)
    def _():
        pl.semaphore_signal(barrier, inc=1, device_id={"tile": tile + 1}, device_id_type=MESH)

    pl.semaphore_wait(barrier, n - 1 + has_up.astype(jnp.int32) + has_down.astype(jnp.int32))

    def remote(src, dst, send_sem, recv_sem, where):
        return pltpu.make_async_remote_copy(
            src_ref=src,
            dst_ref=dst,
            send_sem=send_sem,
            recv_sem=recv_sem,
            device_id=where,
            device_id_type=MESH,
        )

    last = pl.ds(rows - MARGIN, MARGIN)
    first = pl.ds(0, MARGIN)
    second = pl.ds(MARGIN, MARGIN)
    below = pl.ds(rows + MARGIN, MARGIN)
    up = [
        remote(scat.at[:, :, first, :], halo.at[:, :, second, :], halo_send.at[0], halo_recv.at[0], {"tile": tile - 1}),
        remote(pot.at[first, :], phalo.at[second, :], halo_send.at[1], halo_recv.at[1], {"tile": tile - 1}),
    ]
    down = [
        remote(scat.at[:, :, last, :], halo.at[:, :, first, :], halo_send.at[2], halo_recv.at[2], {"tile": tile + 1}),
        remote(pot.at[last, :], phalo.at[first, :], halo_send.at[3], halo_recv.at[3], {"tile": tile + 1}),
    ]

    @pl.when(has_up)
    def _():
        for copy in up:
            copy.start()

    @pl.when(has_down)
    def _():
        for copy in down:
            copy.start()

    @pl.when(tile == 0)
    def _():
        halo[:, :, :MARGIN, :] = jnp.zeros((beams, 2, MARGIN, cols), jnp.float32)
        phalo[:MARGIN, :] = jnp.zeros((MARGIN, cols), jnp.float32)

    @pl.when(tile == tiles - 1)
    def _():
        halo[:, :, MARGIN:, :] = jnp.zeros((beams, 2, MARGIN, cols), jnp.float32)
        phalo[MARGIN:, :] = jnp.zeros((MARGIN, cols), jnp.float32)

    def weights(p):
        corner = row_ref[p] + tile * rows - MARGIN
        picked = index_ref[p]
        result = []
        for b in range(beams):
            turn = (tilt_ref[0, b] * corner + tilt_ref[1, b] * col_ref[p]) & (patch - 1)
            cos, sin = trig_ref[0, turn], trig_ref[1, turn]
            q_re = coef_ref[picked, b]
            q_im = coef_ref[picked + coef_ref.shape[0] // 2, b]
            result.append((q_re * cos + q_im * sin, q_im * cos - q_re * sin))
        return result

    def iota(shape, axis):
        return lax.broadcasted_iota(jnp.int32, shape, axis)

    def ones(mask):
        return jnp.where(mask, 1.0, 0.0).astype(jnp.bfloat16)

    def pick_cols(p):
        shape = (cols, patch)
        return ones(iota(shape, 0) - iota(shape, 1) == col_ref[p])

    def pick_rows(p):
        shape = (patch, rows)
        return ones(iota(shape, 1) - iota(shape, 0) == row_ref[p] - MARGIN)

    def pick_halo(p, out_rows):
        shape = (out_rows, 2 * MARGIN)
        held = iota(shape, 1)
        held = jnp.where(held < MARGIN, held, held + rows)
        wanted = iota(shape, 0)
        if out_rows < patch:
            wanted = jnp.where(wanted < MARGIN, wanted, wanted + middle)
        return ones(held - wanted == row_ref[p])

    def combine(source, count, coefs):
        total_re = total_im = None
        for b in range(beams):
            re = source[b, 0, :count, :]
            im = source[b, 1, :count, :]
            c_re, c_im = coefs[b]
            now_re = c_re * re - c_im * im
            now_im = c_re * im + c_im * re
            total_re = now_re if total_re is None else total_re + now_re
            total_im = now_im if total_im is None else total_im + now_im
        return jnp.concatenate(split(total_re) + split(total_im), 0)

    def block_of(combined, col_pick, row_pick):
        count = combined.shape[0] // 4
        chosen = dot(combined, col_pick).astype(jnp.bfloat16)
        chosen = jnp.concatenate([chosen[: 2 * count], chosen[2 * count :]], 1)
        return dot(jnp.concatenate([row_pick, row_pick], 1), chosen)

    order = list(range(1, n))
    coefs = {}
    col_picks = {}
    copies_a, copies_b = {}, {}
    local[0].wait()
    for k in order + [0]:
        p = lax.rem(me + k, n)
        coefs[k] = weights(p)
        col_picks[k] = pick_cols(p)
        got = block_of(combine(loc, rows, coefs[k]), col_picks[k], pick_rows(p))
        block[k, 0] = got[:, :patch]
        block[k, 1] = got[:, patch:]
        if k != 0:
            copies_a[k] = remote(
                block.at[k, :, pl.ds(MARGIN, middle), :],
                recv_a.at[k - 1],
                a_send.at[k - 1],
                a_recv.at[k - 1],
                {"beam": p},
            )
            copies_a[k].start()

    local[1].wait()

    @pl.when(has_down)
    def _():
        for copy in up:
            copy.wait_recv()

    @pl.when(has_up)
    def _():
        for copy in down:
            copy.wait_recv()

    for k in order + [0]:
        p = lax.rem(me + k, n)
        got = block_of(combine(halo, 2 * MARGIN, coefs[k]), col_picks[k], pick_halo(p, 2 * MARGIN))
        for c in range(2):
            part = got[:, c * patch : (c + 1) * patch]
            send_b[k, c, :MARGIN, :] = block[k, c, :MARGIN, :] + part[:MARGIN]
            send_b[k, c, MARGIN:, :] = block[k, c, MARGIN + middle :, :] + part[MARGIN:]
        if k != 0:
            copies_b[k] = remote(
                send_b.at[k], recv_b.at[k - 1], b_send.at[k - 1], b_recv.at[k - 1], {"beam": p}
            )
            copies_b[k].start()

    tall = jnp.concatenate([ploc[...], phalo[...]], 0)
    high, low = split(tall)
    least = (tall - high.astype(jnp.float32) - low.astype(jnp.float32)).astype(jnp.bfloat16)
    row_pick = jnp.concatenate([pick_rows(me), pick_halo(me, patch)], 1)
    here = None
    for term in (least, low, high):
        now = dot(row_pick, dot(term, col_picks[0]).astype(jnp.bfloat16))
        here = now if here is None else here + now
    here = here * SIGMA_SCALE
    trans[0] = jnp.cos(here)
    trans[1] = jnp.sin(here)

    for k in order:
        copies_a[k].wait_recv()
        copies_b[k].wait_recv()
    local[2].wait()

    parts = []
    for c in range(2):
        mid = block[0, c, MARGIN : MARGIN + middle, :]
        head = send_b[0, c, :MARGIN, :]
        tail = send_b[0, c, MARGIN:, :]
        for k in order:
            mid += recv_a[k - 1, c]
            head += recv_b[k - 1, c, :MARGIN, :]
            tail += recv_b[k - 1, c, MARGIN:, :]
        parts.append(jnp.concatenate([head, mid, tail], 0))
    wave_re, wave_im = parts
    exit_re = trans[0] * wave_re - trans[1] * wave_im
    exit_im = trans[0] * wave_im + trans[1] * wave_re
    ahead = (high_ref[0], low_ref[0])
    back = (high_ref[1], low_ref[1])
    far = transform(jnp.concatenate([exit_re, exit_im], 0), back, ahead)
    far_re, far_im = far[:, :patch], far[:, patch:]
    misfit = far_re * far_re + far_im * far_im - seen[...]
    misfit_ref[...] = misfit
    turned = transform(jnp.concatenate([misfit * far_re, misfit * far_im], 0), ahead, back)
    piece[...] = SIGMA_SCALE * (exit_re * turned[:, patch:] - exit_im * turned[:, :patch])

    copies_p = {}
    for k in order:
        copies_p[k] = remote(
            piece, recv_p.at[k - 1], p_send.at[k - 1], p_recv.at[k - 1], {"beam": lax.rem(me + k, n)}
        )
        copies_p[k].start()

    def place(value, p):
        shape = (patch, cols)
        col_place = ones(iota(shape, 1) - iota(shape, 0) == col_ref[p])
        shape = (rows + 2 * MARGIN, patch)
        row_place = ones(iota(shape, 0) - iota(shape, 1) == row_ref[p])
        moved = dot(jnp.concatenate(split(value), 0), col_place).astype(jnp.bfloat16)
        return dot(jnp.concatenate([row_place, row_place], 1), moved)

    strip[...] = place(piece[...], me)
    for k in order:
        copies_p[k].wait_recv()
        strip[...] += place(recv_p[k - 1], lax.rem(me + n - k, n))

    rim_up = remote(strip.at[first, :], rims.at[1], rim_send.at[0], rim_recv.at[0], {"tile": tile - 1})
    rim_down = remote(strip.at[below, :], rims.at[0], rim_send.at[1], rim_recv.at[1], {"tile": tile + 1})

    @pl.when(has_up)
    def _():
        rim_up.start()

    @pl.when(has_down)
    def _():
        rim_down.start()

    grad_ref[...] = strip[MARGIN : MARGIN + rows, :]

    @pl.when(has_down)
    def _():
        rim_up.wait_recv()
        grad_ref[rows - MARGIN :, :] += rims[1]

    @pl.when(has_up)
    def _():
        rim_down.wait_recv()
        grad_ref[:MARGIN, :] += rims[0]

    for k in order:
        copies_a[k].wait_send()
        copies_b[k].wait_send()
        copies_p[k].wait_send()

    @pl.when(has_up)
    def _():
        for copy in up + [rim_up]:
            copy.wait_send()

    @pl.when(has_down)
    def _():
        for copy in down + [rim_down]:
            copy.wait_send()


def shards(
    n,
    tiles,
    scattering,
    potential,
    row_offset,
    col_offset,
    table_index,
    beam_tilt,
    coef_table,
    measured,
):
    beams, _, rows, cols = scattering.shape
    positions, patch = measured.shape[0], measured.shape[-1]
    assert positions == n and patch & (patch - 1) == 0 and cols & (cols - 1) == 0
    high, low, trig = tables(patch)
    f32 = jnp.float32
    middle = patch - 2 * MARGIN
    smem = pl.BlockSpec(memory_space=pltpu.SMEM)
    vmem = pl.BlockSpec(memory_space=pltpu.VMEM)
    anywhere = pl.BlockSpec(memory_space=pl.ANY)
    strip_rows = rows + 2 * MARGIN
    dma = pltpu.SemaphoreType.DMA
    misfit, grad = pl.pallas_call(
        functools.partial(kernel, n, tiles),
        out_shape=(
            jax.ShapeDtypeStruct((patch, patch), f32),
            jax.ShapeDtypeStruct((rows, cols), f32),
        ),
        in_specs=[smem] * 6 + [vmem] * 2 + [anywhere] * 3,
        out_specs=(vmem, vmem),
        scratch_shapes=[
            pltpu.VMEM((beams, 2, rows, cols), f32),
            pltpu.VMEM((rows, cols), f32),
            pltpu.VMEM((beams, 2, 2 * MARGIN, cols), f32),
            pltpu.VMEM((2 * MARGIN, cols), f32),
            pltpu.VMEM((patch, patch), f32),
            pltpu.VMEM((n, 2, patch, patch), f32),
            pltpu.VMEM((n, 2, 2 * MARGIN, patch), f32),
            pltpu.VMEM((n - 1, 2, middle, patch), f32),
            pltpu.VMEM((n - 1, 2, 2 * MARGIN, patch), f32),
            pltpu.VMEM((2, patch, patch), f32),
            pltpu.VMEM((patch, patch), f32),
            pltpu.VMEM((n - 1, patch, patch), f32),
            pltpu.VMEM((strip_rows, cols), f32),
            pltpu.VMEM((2, MARGIN, cols), f32),
            dma((3,)),
            dma((4,)),
            dma((4,)),
            dma((n - 1,)),
            dma((n - 1,)),
            dma((n - 1,)),
            dma((n - 1,)),
            dma((n - 1,)),
            dma((n - 1,)),
            dma((2,)),
            dma((2,)),
        ],
        compiler_params=pltpu.CompilerParams(
            collective_id=0, has_side_effects=True, vmem_limit_bytes=56 * 1024 * 1024
        ),
    )(
        row_offset[:, 0],
        col_offset[:, 0],
        table_index[:, 0],
        beam_tilt,
        coef_table.reshape(-1, beams),
        trig,
        high,
        low,
        scattering,
        potential,
        measured,
    )
    return misfit[None, None], grad


def solution(mesh):
    in_specs = (
        P("beam", None, "tile", None),
        P("tile", None),
        P(None, "tile"),
        P(None, "tile"),
        P(None, "tile"),
        P(None, "beam"),
        P(None, None, "beam"),
        P(None, "tile", None, None),
    )
    out_specs = (P("beam", "tile", None, None), P("tile", None))
    run = functools.partial(shards, mesh.shape["beam"], mesh.shape["tile"])
    return jax.shard_map(run, mesh=mesh, in_specs=in_specs, out_specs=out_specs, check_vma=False)
```

```python
import functools
import math

import jax
import jax.numpy as jnp
import numpy as np
from jax import lax
from jax.experimental import pallas as pl
from jax.experimental.pallas import tpu as pltpu
from jax.sharding import PartitionSpec as P

MARGIN = 32
SIGMA_SCALE = 1.0
MESH = pl.DeviceIdType.MESH


def tables(length):
    index = np.arange(length)
    angle = (index[:, None] * index[None, :] % length) * (2.0 * math.pi / length)
    re = np.cos(angle) / math.sqrt(length)
    im = -np.sin(angle) / math.sqrt(length)
    ahead = np.block([[re, im], [-im, re]]).astype(np.float32)
    back = np.block([[re, -im], [im, re]]).astype(np.float32)
    both = np.stack([ahead, back])
    high = both.astype(jnp.bfloat16)
    low = (both - high.astype(np.float32)).astype(jnp.bfloat16)
    turns = np.arange(length) * (2.0 * math.pi / length)
    trig = np.stack([np.cos(turns), np.sin(turns)]).astype(np.float32)
    return high, low, trig


def split(value):
    high = value.astype(jnp.bfloat16)
    low = (value - high.astype(jnp.float32)).astype(jnp.bfloat16)
    return high, low


def dot(left, right):
    return jnp.dot(left, right, preferred_element_type=jnp.float32)


def split_dot(left, right):
    return dot(left[0], right[0]) + (dot(left[0], right[1]) + dot(left[1], right[0]))


def transform(stacked, left_table, right_table):
    length = stacked.shape[-1]
    half = split_dot(left_table, split(stacked))
    wide = jnp.concatenate([half[:length], half[length:]], 1)
    return split_dot(split(wide), right_table)


def kernel(
    n,
    tiles,
    row_ref,
    col_ref,
    index_ref,
    tilt_ref,
    coef_ref,
    trig_ref,
    high_ref,
    low_ref,
    scat,
    pot,
    meas,
    misfit_ref,
    grad_ref,
    loc,
    ploc,
    mine,
    from_above,
    from_below,
    edge,
    halo,
    phalo,
    seen,
    block,
    send_b,
    recv_a,
    recv_b,
    trans,
    piece,
    recv_p,
    strip,
    rims,
    local_sem,
    halo_send,
    halo_recv,
    a_send,
    a_recv,
    b_send,
    b_recv,
    p_send,
    p_recv,
    rim_send,
    rim_recv,
):
    me = lax.axis_index("beam")
    tile = lax.axis_index("tile")
    beams = scat.shape[0]
    rows, cols = scat.shape[2], scat.shape[3]
    patch = seen.shape[-1]
    middle = patch - 2 * MARGIN

    local = [
        pltpu.make_async_copy(scat, loc, local_sem.at[0]),
        pltpu.make_async_copy(pot, ploc, local_sem.at[1]),
        pltpu.make_async_copy(meas.at[me, 0], seen, local_sem.at[2]),
    ]
    for copy in local:
        copy.start()

    barrier = pltpu.get_barrier_semaphore()
    for k in range(1, n):
        pl.semaphore_signal(
            barrier, inc=1, device_id={"beam": lax.rem(me + k, n)}, device_id_type=MESH
        )
    has_up = tile > 0
    has_down = tile < tiles - 1

    @pl.when(has_up)
    def _():
        pl.semaphore_signal(barrier, inc=1, device_id={"tile": tile - 1}, device_id_type=MESH)

    @pl.when(has_down)
    def _():
        pl.semaphore_signal(barrier, inc=1, device_id={"tile": tile + 1}, device_id_type=MESH)

    pl.semaphore_wait(barrier, n - 1 + has_up.astype(jnp.int32) + has_down.astype(jnp.int32))

    def remote(src, dst, send_sem, recv_sem, where):
        return pltpu.make_async_remote_copy(
            src_ref=src,
            dst_ref=dst,
            send_sem=send_sem,
            recv_sem=recv_sem,
            device_id=where,
            device_id_type=MESH,
        )

    last = pl.ds(rows - MARGIN, MARGIN)
    first = pl.ds(0, MARGIN)
    second = pl.ds(MARGIN, MARGIN)
    below = pl.ds(rows + MARGIN, MARGIN)
    for p in range(n):
        mine[0, p] = row_ref[p]
        mine[1, p] = col_ref[p]
        mine[2, p] = index_ref[p]
    to_up, to_down = {"tile": tile - 1}, {"tile": tile + 1}
    up = [
        remote(mine, from_below, halo_send.at[0], halo_recv.at[0], to_up),
        remote(pot.at[first, :], phalo.at[second, :], halo_send.at[1], halo_recv.at[1], to_up),
        remote(edge.at[1], halo.at[1], halo_send.at[2], halo_recv.at[2], to_up),
    ]
    down = [
        remote(mine, from_above, halo_send.at[3], halo_recv.at[3], to_down),
        remote(pot.at[last, :], phalo.at[first, :], halo_send.at[4], halo_recv.at[4], to_down),
        remote(edge.at[0], halo.at[0], halo_send.at[5], halo_recv.at[5], to_down),
    ]

    @pl.when(has_up)
    def _():
        up[0].start()
        up[1].start()

    @pl.when(has_down)
    def _():
        down[0].start()
        down[1].start()

    @pl.when(tile == 0)
    def _():
        halo[0] = jnp.zeros(halo.shape[1:], jnp.float32)
        phalo[:MARGIN, :] = jnp.zeros((MARGIN, cols), jnp.float32)

    @pl.when(tile == tiles - 1)
    def _():
        halo[1] = jnp.zeros(halo.shape[1:], jnp.float32)
        phalo[MARGIN:, :] = jnp.zeros((MARGIN, cols), jnp.float32)

    def weights(row_at, col_at, picked, tile_at):
        corner = row_at + tile_at * rows - MARGIN
        result = []
        for b in range(beams):
            turn = (tilt_ref[0, b] * corner + tilt_ref[1, b] * col_at) & (patch - 1)
            cos, sin = trig_ref[0, turn], trig_ref[1, turn]
            q_re = coef_ref[picked, b]
            q_im = coef_ref[picked + coef_ref.shape[0] // 2, b]
            result.append((q_re * cos + q_im * sin, q_im * cos - q_re * sin))
        return result

    def iota(shape, axis):
        return lax.broadcasted_iota(jnp.int32, shape, axis)

    def ones(mask):
        return jnp.where(mask, 1.0, 0.0).astype(jnp.bfloat16)

    def pick_cols(col_at):
        shape = (cols, patch)
        return ones(iota(shape, 0) - iota(shape, 1) == col_at)

    def pick_rows(row_at):
        shape = (patch, rows)
        return ones(iota(shape, 1) - iota(shape, 0) == row_at - MARGIN)

    def pick_halo(row_at):
        shape = (patch, 2 * MARGIN)
        held = iota(shape, 1)
        held = jnp.where(held < MARGIN, held, held + rows)
        return ones(held - iota(shape, 0) == row_at)

    def combine(source, at, count, coefs):
        total_re = total_im = None
        for b in range(beams):
            re = source[b, 0, at : at + count, :]
            im = source[b, 1, at : at + count, :]
            c_re, c_im = coefs[b]
            now_re = c_re * re - c_im * im
            now_im = c_re * im + c_im * re
            total_re = now_re if total_re is None else total_re + now_re
            total_im = now_im if total_im is None else total_im + now_im
        return jnp.concatenate(split(total_re) + split(total_im), 0)

    def block_of(combined, col_pick, row_pick):
        count = combined.shape[0] // 4
        chosen = dot(combined, col_pick).astype(jnp.bfloat16)
        chosen = jnp.concatenate([chosen[: 2 * count], chosen[2 * count :]], 1)
        return dot(jnp.concatenate([row_pick, row_pick], 1), chosen)

    order = list(range(1, n))
    copies_a, copies_b = {}, {}

    def make_block(k):
        p = lax.rem(me + k, n)
        coefs = weights(row_ref[p], col_ref[p], index_ref[p], tile)
        got = block_of(combine(loc, 0, rows, coefs), pick_cols(col_ref[p]), pick_rows(row_ref[p]))
        block[k, 0] = got[:, :patch]
        block[k, 1] = got[:, patch:]

    def make_edge(slot, at, infos, tile_at, first_held, first_row):
        shape = (MARGIN, MARGIN)
        for p in range(n):
            row_at, col_at = infos[0, p], infos[1, p]
            coefs = weights(row_at, col_at, infos[2, p], tile_at)
            shift = iota(shape, 1) - iota(shape, 0) + (first_held - first_row)
            got = block_of(combine(loc, at, MARGIN, coefs), pick_cols(col_at), ones(shift == row_at))
            edge[slot, p, 0] = got[:, :patch]
            edge[slot, p, 1] = got[:, patch:]

    local[0].wait()
    for k in order:
        make_block(k)
        copies_a[k] = remote(
            block.at[k, :, pl.ds(MARGIN, middle), :],
            recv_a.at[k - 1],
            a_send.at[k - 1],
            a_recv.at[k - 1],
            {"beam": lax.rem(me + k, n)},
        )
        copies_a[k].start()

    @pl.when(has_down)
    def _():
        up[0].wait_recv()
        make_edge(0, rows - MARGIN, from_below, tile + 1, 0, 0)
        down[2].start()

    @pl.when(has_up)
    def _():
        down[0].wait_recv()
        make_edge(1, 0, from_above, tile - 1, rows + MARGIN, patch - MARGIN)
        up[2].start()

    make_block(0)
    local[1].wait()

    @pl.when(has_down)
    def _():
        up[1].wait_recv()
        up[2].wait_recv()

    @pl.when(has_up)
    def _():
        down[1].wait_recv()
        down[2].wait_recv()

    for k in order + [0]:
        p = lax.rem(me + k, n)
        for c in range(2):
            send_b[k, c, :MARGIN, :] = block[k, c, :MARGIN, :] + halo[0, p, c]
            send_b[k, c, MARGIN:, :] = block[k, c, MARGIN + middle :, :] + halo[1, p, c]
        if k != 0:
            copies_b[k] = remote(
                send_b.at[k], recv_b.at[k - 1], b_send.at[k - 1], b_recv.at[k - 1], {"beam": p}
            )
            copies_b[k].start()

    tall = jnp.concatenate([ploc[...], phalo[...]], 0)
    high, low = split(tall)
    least = (tall - high.astype(jnp.float32) - low.astype(jnp.float32)).astype(jnp.bfloat16)
    row_pick = jnp.concatenate([pick_rows(row_ref[me]), pick_halo(row_ref[me])], 1)
    own_cols = pick_cols(col_ref[me])
    here = None
    for term in (least, low, high):
        now = dot(row_pick, dot(term, own_cols).astype(jnp.bfloat16))
        here = now if here is None else here + now
    here = here * SIGMA_SCALE
    trans[0] = jnp.cos(here)
    trans[1] = jnp.sin(here)

    for k in order:
        copies_a[k].wait_recv()
        copies_b[k].wait_recv()
    local[2].wait()

    parts = []
    for c in range(2):
        mid = block[0, c, MARGIN : MARGIN + middle, :]
        head = send_b[0, c, :MARGIN, :]
        tail = send_b[0, c, MARGIN:, :]
        for k in order:
            mid += recv_a[k - 1, c]
            head += recv_b[k - 1, c, :MARGIN, :]
            tail += recv_b[k - 1, c, MARGIN:, :]
        parts.append(jnp.concatenate([head, mid, tail], 0))
    wave_re, wave_im = parts
    exit_re = trans[0] * wave_re - trans[1] * wave_im
    exit_im = trans[0] * wave_im + trans[1] * wave_re
    ahead = (high_ref[0], low_ref[0])
    back = (high_ref[1], low_ref[1])
    far = transform(jnp.concatenate([exit_re, exit_im], 0), back, ahead)
    far_re, far_im = far[:, :patch], far[:, patch:]
    misfit = far_re * far_re + far_im * far_im - seen[...]
    misfit_ref[...] = misfit
    turned = transform(jnp.concatenate([misfit * far_re, misfit * far_im], 0), ahead, back)
    piece[...] = SIGMA_SCALE * (exit_re * turned[:, patch:] - exit_im * turned[:, :patch])

    copies_p = {}
    for k in order:
        copies_p[k] = remote(
            piece, recv_p.at[k - 1], p_send.at[k - 1], p_recv.at[k - 1], {"beam": lax.rem(me + k, n)}
        )
        copies_p[k].start()

    def place(value, p):
        shape = (patch, cols)
        col_place = ones(iota(shape, 1) - iota(shape, 0) == col_ref[p])
        shape = (rows + 2 * MARGIN, patch)
        row_place = ones(iota(shape, 0) - iota(shape, 1) == row_ref[p])
        moved = dot(jnp.concatenate(split(value), 0), col_place).astype(jnp.bfloat16)
        return dot(jnp.concatenate([row_place, row_place], 1), moved)

    strip[...] = place(piece[...], me)
    for k in order:
        copies_p[k].wait_recv()
        strip[...] += place(recv_p[k - 1], lax.rem(me + n - k, n))

    rim_up = remote(strip.at[first, :], rims.at[1], rim_send.at[0], rim_recv.at[0], {"tile": tile - 1})
    rim_down = remote(strip.at[below, :], rims.at[0], rim_send.at[1], rim_recv.at[1], {"tile": tile + 1})

    @pl.when(has_up)
    def _():
        rim_up.start()

    @pl.when(has_down)
    def _():
        rim_down.start()

    grad_ref[...] = strip[MARGIN : MARGIN + rows, :]

    @pl.when(has_down)
    def _():
        rim_up.wait_recv()
        grad_ref[rows - MARGIN :, :] += rims[1]

    @pl.when(has_up)
    def _():
        rim_down.wait_recv()
        grad_ref[:MARGIN, :] += rims[0]

    for k in order:
        copies_a[k].wait_send()
        copies_b[k].wait_send()
        copies_p[k].wait_send()

    @pl.when(has_up)
    def _():
        for copy in up + [rim_up]:
            copy.wait_send()

    @pl.when(has_down)
    def _():
        for copy in down + [rim_down]:
            copy.wait_send()


def hand_over(misfit, grad, misfit_out, grad_out, sem):
    copies = [
        pltpu.make_async_copy(misfit, misfit_out, sem.at[0]),
        pltpu.make_async_copy(grad, grad_out, sem.at[1]),
    ]
    for copy in copies:
        copy.start()
    for copy in copies:
        copy.wait()


def shards(
    n,
    tiles,
    scattering,
    potential,
    row_offset,
    col_offset,
    table_index,
    beam_tilt,
    coef_table,
    measured,
):
    beams, _, rows, cols = scattering.shape
    positions, patch = measured.shape[0], measured.shape[-1]
    assert positions == n and patch & (patch - 1) == 0 and cols & (cols - 1) == 0
    high, low, trig = tables(patch)
    f32 = jnp.float32
    middle = patch - 2 * MARGIN
    smem = pl.BlockSpec(memory_space=pltpu.SMEM)
    vmem = pl.BlockSpec(memory_space=pltpu.VMEM)
    anywhere = pl.BlockSpec(memory_space=pl.ANY)
    strip_rows = rows + 2 * MARGIN
    dma = pltpu.SemaphoreType.DMA
    misfit, grad = pl.pallas_call(
        functools.partial(kernel, n, tiles),
        out_shape=(
            jax.ShapeDtypeStruct((patch, patch), f32),
            jax.ShapeDtypeStruct((rows, cols), f32),
        ),
        in_specs=[smem] * 6 + [vmem] * 2 + [anywhere] * 3,
        out_specs=(vmem, vmem),
        scratch_shapes=[
            pltpu.VMEM((beams, 2, rows, cols), f32),
            pltpu.VMEM((rows, cols), f32),
            pltpu.SMEM((3, n), jnp.int32),
            pltpu.SMEM((3, n), jnp.int32),
            pltpu.SMEM((3, n), jnp.int32),
            pltpu.VMEM((2, n, 2, MARGIN, patch), f32),
            pltpu.VMEM((2, n, 2, MARGIN, patch), f32),
            pltpu.VMEM((2 * MARGIN, cols), f32),
            pltpu.VMEM((patch, patch), f32),
            pltpu.VMEM((n, 2, patch, patch), f32),
            pltpu.VMEM((n, 2, 2 * MARGIN, patch), f32),
            pltpu.VMEM((n - 1, 2, middle, patch), f32),
            pltpu.VMEM((n - 1, 2, 2 * MARGIN, patch), f32),
            pltpu.VMEM((2, patch, patch), f32),
            pltpu.VMEM((patch, patch), f32),
            pltpu.VMEM((n - 1, patch, patch), f32),
            pltpu.VMEM((strip_rows, cols), f32),
            pltpu.VMEM((2, MARGIN, cols), f32),
            dma((3,)),
            dma((6,)),
            dma((6,)),
            dma((n - 1,)),
            dma((n - 1,)),
            dma((n - 1,)),
            dma((n - 1,)),
            dma((n - 1,)),
            dma((n - 1,)),
            dma((2,)),
            dma((2,)),
        ],
        compiler_params=pltpu.CompilerParams(
            collective_id=0, has_side_effects=True, vmem_limit_bytes=56 * 1024 * 1024
        ),
    )(
        row_offset[:, 0],
        col_offset[:, 0],
        table_index[:, 0],
        beam_tilt,
        coef_table.reshape(-1, beams),
        trig,
        high,
        low,
        scattering,
        potential,
        measured,
    )
    misfit, grad = pl.pallas_call(
        hand_over,
        out_shape=(
            jax.ShapeDtypeStruct((patch, patch), f32),
            jax.ShapeDtypeStruct((rows, cols), f32),
        ),
        in_specs=[anywhere] * 2,
        out_specs=(anywhere, anywhere),
        scratch_shapes=[dma((2,))],
        compiler_params=pltpu.CompilerParams(vmem_limit_bytes=56 * 1024 * 1024),
    )(misfit, grad)
    return misfit[None, None], grad


def solution(mesh):
    in_specs = (
        P("beam", None, "tile", None),
        P("tile", None),
        P(None, "tile"),
        P(None, "tile"),
        P(None, "tile"),
        P(None, "beam"),
        P(None, None, "beam"),
        P(None, "tile", None, None),
    )
    out_specs = (P("beam", "tile", None, None), P("tile", None))
    run = functools.partial(shards, mesh.shape["beam"], mesh.shape["tile"])
    return jax.shard_map(run, mesh=mesh, in_specs=in_specs, out_specs=out_specs, check_vma=False)
```

```python
import functools
import math

import jax
import jax.numpy as jnp
import numpy as np
from jax import lax
from jax.experimental import pallas as pl
from jax.experimental.pallas import tpu as pltpu
from jax.sharding import PartitionSpec as P

MARGIN = 32
SIGMA_SCALE = 1.0
MESH = pl.DeviceIdType.MESH


def tables(length):
    index = np.arange(length)
    angle = (index[:, None] * index[None, :] % length) * (2.0 * math.pi / length)
    re = np.cos(angle) / math.sqrt(length)
    im = -np.sin(angle) / math.sqrt(length)
    ahead = np.block([[re, im], [-im, re]]).astype(np.float32)
    back = np.block([[re, -im], [im, re]]).astype(np.float32)
    both = np.stack([ahead, back])
    high = both.astype(jnp.bfloat16)
    low = (both - high.astype(np.float32)).astype(jnp.bfloat16)
    turns = np.arange(length) * (2.0 * math.pi / length)
    trig = np.stack([np.cos(turns), np.sin(turns)]).astype(np.float32)
    return high, low, trig


def split(value):
    high = value.astype(jnp.bfloat16)
    low = (value - high.astype(jnp.float32)).astype(jnp.bfloat16)
    return high, low


def dot(left, right):
    return jnp.dot(left, right, preferred_element_type=jnp.float32)


def split_dot(left, right):
    return dot(left[0], right[0]) + (dot(left[0], right[1]) + dot(left[1], right[0]))


def transform(stacked, left_table, right_table):
    length = stacked.shape[-1]
    half = split_dot(left_table, split(stacked))
    wide = jnp.concatenate([half[:length], half[length:]], 1)
    return split_dot(split(wide), right_table)


def kernel(
    n,
    tiles,
    row_ref,
    col_ref,
    index_ref,
    tilt_ref,
    coef_ref,
    trig_ref,
    high_ref,
    low_ref,
    scat,
    pot,
    meas,
    power_ref,
    core_ref,
    extra_ref,
    loc,
    ploc,
    mine,
    from_above,
    from_below,
    edge,
    halo,
    phalo,
    seen,
    block,
    send_b,
    recv_a,
    recv_b,
    relay_a,
    relay_b,
    trans,
    piece,
    recv_p,
    strip,
    rims,
    local_sem,
    halo_send,
    halo_recv,
    a_send,
    a_recv,
    b_send,
    b_recv,
    p_send,
    p_recv,
    rim_send,
    rim_recv,
    relay_recv,
    forward_send,
):
    me = lax.axis_index("beam")
    tile = lax.axis_index("tile")
    beams = scat.shape[0]
    rows, cols = scat.shape[2], scat.shape[3]
    patch = seen.shape[-1]
    middle = patch - 2 * MARGIN

    local = [
        pltpu.make_async_copy(scat, loc, local_sem.at[0]),
        pltpu.make_async_copy(pot, ploc, local_sem.at[1]),
        pltpu.make_async_copy(meas.at[me, 0], seen, local_sem.at[2]),
    ]
    for copy in local:
        copy.start()

    barrier = pltpu.get_barrier_semaphore()
    for k in range(1, n):
        pl.semaphore_signal(
            barrier, inc=1, device_id={"beam": lax.rem(me + k, n)}, device_id_type=MESH
        )
    has_up = tile > 0
    has_down = tile < tiles - 1

    @pl.when(has_up)
    def _():
        pl.semaphore_signal(barrier, inc=1, device_id={"tile": tile - 1}, device_id_type=MESH)

    @pl.when(has_down)
    def _():
        pl.semaphore_signal(barrier, inc=1, device_id={"tile": tile + 1}, device_id_type=MESH)

    pl.semaphore_wait(barrier, n - 1 + has_up.astype(jnp.int32) + has_down.astype(jnp.int32))

    def remote(src, dst, send_sem, recv_sem, where):
        return pltpu.make_async_remote_copy(
            src_ref=src,
            dst_ref=dst,
            send_sem=send_sem,
            recv_sem=recv_sem,
            device_id=where,
            device_id_type=MESH,
        )

    last = pl.ds(rows - MARGIN, MARGIN)
    first = pl.ds(0, MARGIN)
    second = pl.ds(MARGIN, MARGIN)
    below = pl.ds(rows + MARGIN, MARGIN)
    for p in range(n):
        mine[0, p] = row_ref[p]
        mine[1, p] = col_ref[p]
        mine[2, p] = index_ref[p]
    to_up, to_down = {"tile": tile - 1}, {"tile": tile + 1}
    up = [
        remote(mine, from_below, halo_send.at[0], halo_recv.at[0], to_up),
        remote(pot.at[first, :], phalo.at[second, :], halo_send.at[1], halo_recv.at[1], to_up),
        remote(edge.at[1], halo.at[1], halo_send.at[2], halo_recv.at[2], to_up),
    ]
    down = [
        remote(mine, from_above, halo_send.at[3], halo_recv.at[3], to_down),
        remote(pot.at[last, :], phalo.at[first, :], halo_send.at[4], halo_recv.at[4], to_down),
        remote(edge.at[0], halo.at[0], halo_send.at[5], halo_recv.at[5], to_down),
    ]

    @pl.when(has_up)
    def _():
        up[0].start()
        up[1].start()

    @pl.when(has_down)
    def _():
        down[0].start()
        down[1].start()

    @pl.when(tile == 0)
    def _():
        halo[0] = jnp.zeros(halo.shape[1:], jnp.float32)
        phalo[:MARGIN, :] = jnp.zeros((MARGIN, cols), jnp.float32)

    @pl.when(tile == tiles - 1)
    def _():
        halo[1] = jnp.zeros(halo.shape[1:], jnp.float32)
        phalo[MARGIN:, :] = jnp.zeros((MARGIN, cols), jnp.float32)

    def weights(row_at, col_at, picked, tile_at):
        corner = row_at + tile_at * rows - MARGIN
        result = []
        for b in range(beams):
            turn = (tilt_ref[0, b] * corner + tilt_ref[1, b] * col_at) & (patch - 1)
            cos, sin = trig_ref[0, turn], trig_ref[1, turn]
            q_re = coef_ref[picked, b]
            q_im = coef_ref[picked + coef_ref.shape[0] // 2, b]
            result.append((q_re * cos + q_im * sin, q_im * cos - q_re * sin))
        return result

    def iota(shape, axis):
        return lax.broadcasted_iota(jnp.int32, shape, axis)

    def ones(mask):
        return jnp.where(mask, 1.0, 0.0).astype(jnp.bfloat16)

    def pick_cols(col_at):
        shape = (cols, patch)
        return ones(iota(shape, 0) - iota(shape, 1) == col_at)

    def pick_rows(row_at):
        shape = (patch, rows)
        return ones(iota(shape, 1) - iota(shape, 0) == row_at - MARGIN)

    def pick_halo(row_at):
        shape = (patch, 2 * MARGIN)
        held = iota(shape, 1)
        held = jnp.where(held < MARGIN, held, held + rows)
        return ones(held - iota(shape, 0) == row_at)

    def combine(source, at, count, coefs):
        total_re = total_im = None
        for b in range(beams):
            re = source[b, 0, at : at + count, :]
            im = source[b, 1, at : at + count, :]
            c_re, c_im = coefs[b]
            now_re = c_re * re - c_im * im
            now_im = c_re * im + c_im * re
            total_re = now_re if total_re is None else total_re + now_re
            total_im = now_im if total_im is None else total_im + now_im
        return jnp.concatenate(split(total_re) + split(total_im), 0)

    def block_of(combined, col_pick, row_pick):
        count = combined.shape[0] // 4
        chosen = dot(combined, col_pick).astype(jnp.bfloat16)
        chosen = jnp.concatenate([chosen[: 2 * count], chosen[2 * count :]], 1)
        return dot(jnp.concatenate([row_pick, row_pick], 1), chosen)

    order = list(range(1, n))
    copies_a, copies_b = {}, {}

    def make_block(k):
        p = lax.rem(me + k, n)
        coefs = weights(row_ref[p], col_ref[p], index_ref[p], tile)
        got = block_of(combine(loc, 0, rows, coefs), pick_cols(col_ref[p]), pick_rows(row_ref[p]))
        block[k, 0] = got[:, :patch]
        block[k, 1] = got[:, patch:]

    def make_edge(slot, at, infos, tile_at, first_held, first_row):
        shape = (MARGIN, MARGIN)
        for p in range(n):
            row_at, col_at = infos[0, p], infos[1, p]
            coefs = weights(row_at, col_at, infos[2, p], tile_at)
            shift = iota(shape, 1) - iota(shape, 0) + (first_held - first_row)
            got = block_of(combine(loc, at, MARGIN, coefs), pick_cols(col_at), ones(shift == row_at))
            edge[slot, p, 0] = got[:, :patch]
            edge[slot, p, 1] = got[:, patch:]

    def normal(k, src, dst, send_sem, recv_sem):
        return remote(
            src, dst.at[k - 1], send_sem.at[k - 1], recv_sem.at[k - 1], {"beam": lax.rem(me + k, n)}
        )

    def detour(k, src, relay, send_sem, relay_sem):
        there = 1 if k == n - 1 else n - 2
        return remote(src, relay, send_sem.at[k - 1], relay_sem, {"beam": there})

    def ship(k, src, dst, relay, send_sem, recv_sem, relay_sem):
        straight = normal(k, src, dst, send_sem, recv_sem)
        if k in (1, n - 1):
            at_end = me == (0 if k == n - 1 else n - 1)

            @pl.when(at_end)
            def _():
                detour(k, src, relay, send_sem, relay_sem).start()

            @pl.when(jnp.logical_not(at_end))
            def _():
                straight.start()
        else:
            straight.start()
        return straight

    def add_relayed(k, src, relay, send_sem, relay_sem):
        for spot, where in ((n - 2, 1), (2, n - 2)):
            if k == spot:

                @pl.when(me == where)
                def _():
                    detour(1, src, relay, send_sem, relay_sem).wait_recv()
                    src[...] += relay[...]

    def take(k, copy):
        if k in (1, n - 1):

            @pl.when(me != (n - 1 if k == n - 1 else 0))
            def _():
                copy.wait_recv()
        else:
            copy.wait_recv()

    for k, where in ((n - 1, n - 1), (1, 0)):

        @pl.when(me == where)
        def _():
            recv_a[k - 1] = jnp.zeros(recv_a.shape[1:], jnp.float32)
            recv_b[k - 1] = jnp.zeros(recv_b.shape[1:], jnp.float32)

    local[0].wait()
    order = [n - 1, 1] + list(range(2, n - 1))
    for k in order:
        make_block(k)
        src = block.at[k, :, pl.ds(MARGIN, middle), :]
        add_relayed(k, src, relay_a, a_send, relay_recv.at[0])
        copies_a[k] = ship(k, src, recv_a, relay_a, a_send, a_recv, relay_recv.at[0])

    @pl.when(has_down)
    def _():
        up[0].wait_recv()
        make_edge(0, rows - MARGIN, from_below, tile + 1, 0, 0)
        down[2].start()

    @pl.when(has_up)
    def _():
        down[0].wait_recv()
        make_edge(1, 0, from_above, tile - 1, rows + MARGIN, patch - MARGIN)
        up[2].start()

    make_block(0)
    local[1].wait()

    @pl.when(has_down)
    def _():
        up[1].wait_recv()
        up[2].wait_recv()

    @pl.when(has_up)
    def _():
        down[1].wait_recv()
        down[2].wait_recv()

    for k in order + [0]:
        p = lax.rem(me + k, n)
        for c in range(2):
            send_b[k, c, :MARGIN, :] = block[k, c, :MARGIN, :] + halo[0, p, c]
            send_b[k, c, MARGIN:, :] = block[k, c, MARGIN + middle :, :] + halo[1, p, c]
        if k != 0:
            src = send_b.at[k]
            add_relayed(k, src, relay_b, b_send, relay_recv.at[1])
            copies_b[k] = ship(k, src, recv_b, relay_b, b_send, b_recv, relay_recv.at[1])

    tall = jnp.concatenate([ploc[...], phalo[...]], 0)
    high, low = split(tall)
    least = (tall - high.astype(jnp.float32) - low.astype(jnp.float32)).astype(jnp.bfloat16)
    row_pick = jnp.concatenate([pick_rows(row_ref[me]), pick_halo(row_ref[me])], 1)
    own_cols = pick_cols(col_ref[me])
    here = None
    for term in (least, low, high):
        now = dot(row_pick, dot(term, own_cols).astype(jnp.bfloat16))
        here = now if here is None else here + now
    here = here * SIGMA_SCALE
    trans[0] = jnp.cos(here)
    trans[1] = jnp.sin(here)

    for k in order:
        take(k, copies_a[k])
        take(k, copies_b[k])
    local[2].wait()

    parts = []
    for c in range(2):
        mid = block[0, c, MARGIN : MARGIN + middle, :]
        head = send_b[0, c, :MARGIN, :]
        tail = send_b[0, c, MARGIN:, :]
        for k in order:
            mid += recv_a[k - 1, c]
            head += recv_b[k - 1, c, :MARGIN, :]
            tail += recv_b[k - 1, c, MARGIN:, :]
        parts.append(jnp.concatenate([head, mid, tail], 0))
    wave_re, wave_im = parts
    exit_re = trans[0] * wave_re - trans[1] * wave_im
    exit_im = trans[0] * wave_im + trans[1] * wave_re
    ahead = (high_ref[0], low_ref[0])
    back = (high_ref[1], low_ref[1])
    far = transform(jnp.concatenate([exit_re, exit_im], 0), back, ahead)
    far_re, far_im = far[:, :patch], far[:, patch:]
    power = far_re * far_re + far_im * far_im
    power_ref[...] = power
    misfit = power - seen[...]
    turned = transform(jnp.concatenate([misfit * far_re, misfit * far_im], 0), ahead, back)
    piece[...] = SIGMA_SCALE * (exit_re * turned[:, patch:] - exit_im * turned[:, :patch])

    copies_p = {}
    order = list(range(2, n - 1)) + [1, n - 1]
    for k in order:
        copies_p[k] = normal(k, piece, recv_p, p_send, p_recv)
        if k in (1, n - 1):

            @pl.when(me != (0 if k == n - 1 else n - 1))
            def _():
                copies_p[k].start()
        else:
            copies_p[k].start()
    forwards = [
        (n - 2, n - 2, remote(recv_p.at[n - 3], recv_p.at[n - 2], forward_send, p_recv.at[n - 2], {"beam": n - 1})),
        (1, 2, remote(recv_p.at[1], recv_p.at[0], forward_send, p_recv.at[0], {"beam": 0})),
    ]

    def place(value, p):
        shape = (patch, cols)
        col_place = ones(iota(shape, 1) - iota(shape, 0) == col_ref[p])
        shape = (rows + 2 * MARGIN, patch)
        row_place = ones(iota(shape, 0) - iota(shape, 1) == row_ref[p])
        moved = dot(jnp.concatenate(split(value), 0), col_place).astype(jnp.bfloat16)
        return dot(jnp.concatenate([row_place, row_place], 1), moved)

    strip[...] = place(piece[...], me)
    for k in order:
        copies_p[k].wait_recv()
        for where, spot, copy in forwards:
            if k == spot:
                pl.when(me == where)(copy.start)
        strip[...] += place(recv_p[k - 1], lax.rem(me + n - k, n))

    rim_up = remote(strip.at[first, :], rims.at[1], rim_send.at[0], rim_recv.at[0], {"tile": tile - 1})
    rim_down = remote(strip.at[below, :], rims.at[0], rim_send.at[1], rim_recv.at[1], {"tile": tile + 1})

    @pl.when(has_up)
    def _():
        rim_up.start()

    @pl.when(has_down)
    def _():
        rim_down.start()

    core_ref[...] = strip[MARGIN : MARGIN + rows, :]
    extra_ref[...] = jnp.zeros(extra_ref.shape, jnp.float32)

    @pl.when(has_down)
    def _():
        rim_up.wait_recv()
        extra_ref[rows - MARGIN :, :] = rims[1]

    @pl.when(has_up)
    def _():
        rim_down.wait_recv()
        extra_ref[:MARGIN, :] = rims[0]

    for k in order:
        copies_a[k].wait_send()
        copies_b[k].wait_send()
        if k in (1, n - 1):
            pl.when(me != (0 if k == n - 1 else n - 1))(copies_p[k].wait_send)
        else:
            copies_p[k].wait_send()
    for where, _, copy in forwards:
        pl.when(me == where)(copy.wait_send)

    @pl.when(has_up)
    def _():
        for copy in up + [rim_up]:
            copy.wait_send()

    @pl.when(has_down)
    def _():
        for copy in down + [rim_down]:
            copy.wait_send()


def shards(
    n,
    tiles,
    scattering,
    potential,
    row_offset,
    col_offset,
    table_index,
    beam_tilt,
    coef_table,
    measured,
):
    beams, _, rows, cols = scattering.shape
    positions, patch = measured.shape[0], measured.shape[-1]
    assert positions == n and n >= 4 and patch & (patch - 1) == 0 and cols & (cols - 1) == 0
    high, low, trig = tables(patch)
    f32 = jnp.float32
    middle = patch - 2 * MARGIN
    smem = pl.BlockSpec(memory_space=pltpu.SMEM)
    vmem = pl.BlockSpec(memory_space=pltpu.VMEM)
    anywhere = pl.BlockSpec(memory_space=pl.ANY)
    strip_rows = rows + 2 * MARGIN
    dma = pltpu.SemaphoreType.DMA
    power, core, extra = pl.pallas_call(
        functools.partial(kernel, n, tiles),
        out_shape=(
            jax.ShapeDtypeStruct((patch, patch), f32),
            jax.ShapeDtypeStruct((rows, cols), f32),
            jax.ShapeDtypeStruct((rows, cols), f32),
        ),
        in_specs=[smem] * 6 + [vmem] * 2 + [anywhere] * 3,
        out_specs=(vmem, vmem, vmem),
        scratch_shapes=[
            pltpu.VMEM((beams, 2, rows, cols), f32),
            pltpu.VMEM((rows, cols), f32),
            pltpu.SMEM((3, n), jnp.int32),
            pltpu.SMEM((3, n), jnp.int32),
            pltpu.SMEM((3, n), jnp.int32),
            pltpu.VMEM((2, n, 2, MARGIN, patch), f32),
            pltpu.VMEM((2, n, 2, MARGIN, patch), f32),
            pltpu.VMEM((2 * MARGIN, cols), f32),
            pltpu.VMEM((patch, patch), f32),
            pltpu.VMEM((n, 2, patch, patch), f32),
            pltpu.VMEM((n, 2, 2 * MARGIN, patch), f32),
            pltpu.VMEM((n - 1, 2, middle, patch), f32),
            pltpu.VMEM((n - 1, 2, 2 * MARGIN, patch), f32),
            pltpu.VMEM((2, middle, patch), f32),
            pltpu.VMEM((2, 2 * MARGIN, patch), f32),
            pltpu.VMEM((2, patch, patch), f32),
            pltpu.VMEM((patch, patch), f32),
            pltpu.VMEM((n - 1, patch, patch), f32),
            pltpu.VMEM((strip_rows, cols), f32),
            pltpu.VMEM((2, MARGIN, cols), f32),
            dma((3,)),
            dma((6,)),
            dma((6,)),
            dma((n - 1,)),
            dma((n - 1,)),
            dma((n - 1,)),
            dma((n - 1,)),
            dma((n - 1,)),
            dma((n - 1,)),
            dma((2,)),
            dma((2,)),
            dma((2,)),
            dma,
        ],
        compiler_params=pltpu.CompilerParams(
            collective_id=0, has_side_effects=True, vmem_limit_bytes=56 * 1024 * 1024
        ),
    )(
        row_offset[:, 0],
        col_offset[:, 0],
        table_index[:, 0],
        beam_tilt,
        coef_table.reshape(-1, beams),
        trig,
        high,
        low,
        scattering,
        potential,
        measured,
    )
    seen = lax.dynamic_index_in_dim(measured, lax.axis_index("beam"), 0, keepdims=True)
    return power[None, None] - seen, core + extra


def solution(mesh):
    in_specs = (
        P("beam", None, "tile", None),
        P("tile", None),
        P(None, "tile"),
        P(None, "tile"),
        P(None, "tile"),
        P(None, "beam"),
        P(None, None, "beam"),
        P(None, "tile", None, None),
    )
    out_specs = (P("beam", "tile", None, None), P("tile", None))
    run = functools.partial(shards, mesh.shape["beam"], mesh.shape["tile"])
    return jax.shard_map(run, mesh=mesh, in_specs=in_specs, out_specs=out_specs, check_vma=False)
```

```python
import functools
import math

import jax
import jax.numpy as jnp
import numpy as np
from jax import lax
from jax.experimental import pallas as pl
from jax.experimental.pallas import tpu as pltpu
from jax.sharding import PartitionSpec as P

MARGIN = 32
SIGMA_SCALE = 1.0
MESH = pl.DeviceIdType.MESH


def tables(length):
    index = np.arange(length)
    angle = (index[:, None] * index[None, :] % length) * (2.0 * math.pi / length)
    re = np.cos(angle) / math.sqrt(length)
    im = -np.sin(angle) / math.sqrt(length)
    ahead = np.block([[re, im], [-im, re]]).astype(np.float32)
    back = np.block([[re, -im], [im, re]]).astype(np.float32)
    both = np.stack([ahead, back])
    high = both.astype(jnp.bfloat16)
    low = (both - high.astype(np.float32)).astype(jnp.bfloat16)
    turns = np.arange(length) * (2.0 * math.pi / length)
    trig = np.stack([np.cos(turns), np.sin(turns)]).astype(np.float32)
    return high, low, trig


def split(value):
    high = value.astype(jnp.bfloat16)
    low = (value - high.astype(jnp.float32)).astype(jnp.bfloat16)
    return high, low


def dot(left, right):
    return jnp.dot(left, right, preferred_element_type=jnp.float32)


def split_dot(left, right):
    return dot(left[0], right[0]) + (dot(left[0], right[1]) + dot(left[1], right[0]))


def transform(stacked, left_table, right_table):
    length = stacked.shape[-1]
    half = split_dot(left_table, split(stacked))
    wide = jnp.concatenate([half[:length], half[length:]], 1)
    return split_dot(split(wide), right_table)


def kernel(
    n,
    tiles,
    row_ref,
    col_ref,
    index_ref,
    tilt_ref,
    coef_ref,
    trig_ref,
    high_ref,
    low_ref,
    scat,
    pot,
    meas,
    misfit_ref,
    grad_ref,
    loc,
    ploc,
    mine,
    from_above,
    from_below,
    edge,
    halo,
    phalo,
    seen,
    block,
    send_b,
    recv_a,
    recv_b,
    trans,
    piece,
    recv_p,
    strip,
    rims,
    local_sem,
    halo_send,
    halo_recv,
    a_send,
    a_recv,
    b_send,
    b_recv,
    p_send,
    p_recv,
    rim_send,
    rim_recv,
):
    me = lax.axis_index("beam")
    tile = lax.axis_index("tile")
    beams = scat.shape[0]
    rows, cols = scat.shape[2], scat.shape[3]
    patch = seen.shape[-1]
    middle = patch - 2 * MARGIN

    local = [
        pltpu.make_async_copy(scat, loc, local_sem.at[0]),
        pltpu.make_async_copy(pot, ploc, local_sem.at[1]),
        pltpu.make_async_copy(meas.at[me, 0], seen, local_sem.at[2]),
    ]
    for copy in local:
        copy.start()

    barrier = pltpu.get_barrier_semaphore()
    for k in range(1, n):
        pl.semaphore_signal(
            barrier, inc=1, device_id={"beam": lax.rem(me + k, n)}, device_id_type=MESH
        )
    has_up = tile > 0
    has_down = tile < tiles - 1

    @pl.when(has_up)
    def _():
        pl.semaphore_signal(barrier, inc=1, device_id={"tile": tile - 1}, device_id_type=MESH)

    @pl.when(has_down)
    def _():
        pl.semaphore_signal(barrier, inc=1, device_id={"tile": tile + 1}, device_id_type=MESH)

    pl.semaphore_wait(barrier, n - 1 + has_up.astype(jnp.int32) + has_down.astype(jnp.int32))

    def remote(src, dst, send_sem, recv_sem, where):
        return pltpu.make_async_remote_copy(
            src_ref=src,
            dst_ref=dst,
            send_sem=send_sem,
            recv_sem=recv_sem,
            device_id=where,
            device_id_type=MESH,
        )

    last = pl.ds(rows - MARGIN, MARGIN)
    first = pl.ds(0, MARGIN)
    second = pl.ds(MARGIN, MARGIN)
    below = pl.ds(rows + MARGIN, MARGIN)
    for p in range(n):
        mine[0, p] = row_ref[p]
        mine[1, p] = col_ref[p]
        mine[2, p] = index_ref[p]
    to_up, to_down = {"tile": tile - 1}, {"tile": tile + 1}
    up = [
        remote(mine, from_below, halo_send.at[0], halo_recv.at[0], to_up),
        remote(pot.at[first, :], phalo.at[second, :], halo_send.at[1], halo_recv.at[1], to_up),
        remote(edge.at[1], halo.at[1], halo_send.at[2], halo_recv.at[2], to_up),
    ]
    down = [
        remote(mine, from_above, halo_send.at[3], halo_recv.at[3], to_down),
        remote(pot.at[last, :], phalo.at[first, :], halo_send.at[4], halo_recv.at[4], to_down),
        remote(edge.at[0], halo.at[0], halo_send.at[5], halo_recv.at[5], to_down),
    ]

    @pl.when(has_up)
    def _():
        up[0].start()
        up[1].start()

    @pl.when(has_down)
    def _():
        down[0].start()
        down[1].start()

    @pl.when(tile == 0)
    def _():
        halo[0] = jnp.zeros(halo.shape[1:], jnp.float32)
        for i in range(3):
            for p in range(n):
                from_above[i, p] = 0
        phalo[:MARGIN, :] = jnp.zeros((MARGIN, cols), jnp.float32)

    @pl.when(tile == tiles - 1)
    def _():
        halo[1] = jnp.zeros(halo.shape[1:], jnp.float32)
        for i in range(3):
            for p in range(n):
                from_below[i, p] = 0
        phalo[MARGIN:, :] = jnp.zeros((MARGIN, cols), jnp.float32)

    def weights(row_at, col_at, picked, tile_at):
        corner = row_at + tile_at * rows - MARGIN
        result = []
        for b in range(beams):
            turn = (tilt_ref[0, b] * corner + tilt_ref[1, b] * col_at) & (patch - 1)
            cos, sin = trig_ref[0, turn], trig_ref[1, turn]
            q_re = coef_ref[picked, b]
            q_im = coef_ref[picked + coef_ref.shape[0] // 2, b]
            result.append((q_re * cos + q_im * sin, q_im * cos - q_re * sin))
        return result

    def iota(shape, axis):
        return lax.broadcasted_iota(jnp.int32, shape, axis)

    def ones(mask):
        return jnp.where(mask, 1.0, 0.0).astype(jnp.bfloat16)

    def pick_cols(col_at):
        shape = (cols, patch)
        return ones(iota(shape, 0) - iota(shape, 1) == col_at)

    def pick_rows(row_at):
        shape = (patch, rows)
        return ones(iota(shape, 1) - iota(shape, 0) == row_at - MARGIN)

    def pick_halo(row_at):
        shape = (patch, 2 * MARGIN)
        held = iota(shape, 1)
        held = jnp.where(held < MARGIN, held, held + rows)
        return ones(held - iota(shape, 0) == row_at)

    def combine(source, at, count, coefs):
        total_re = total_im = None
        for b in range(beams):
            re = source[b, 0, at : at + count, :]
            im = source[b, 1, at : at + count, :]
            c_re, c_im = coefs[b]
            now_re = c_re * re - c_im * im
            now_im = c_re * im + c_im * re
            total_re = now_re if total_re is None else total_re + now_re
            total_im = now_im if total_im is None else total_im + now_im
        return jnp.concatenate(split(total_re) + split(total_im), 0)

    def blocks_of(jobs):
        sums = [combine(source, at, count, coefs) for source, at, count, coefs, _, _ in jobs]
        chosen = [dot(total, job[4]).astype(jnp.bfloat16) for total, job in zip(sums, jobs)]
        results = []
        for pair, job in zip(chosen, jobs):
            count = 2 * job[2]
            pair = jnp.concatenate([pair[:count], pair[count:]], 1)
            results.append(dot(jnp.concatenate([job[5], job[5]], 1), pair))
        return results

    def block_job(k):
        p = lax.rem(me + k, n)
        coefs = weights(row_ref[p], col_ref[p], index_ref[p], tile)
        return loc, 0, rows, coefs, pick_cols(col_ref[p]), pick_rows(row_ref[p])

    def edge_job(p, at, infos, tile_at, first_held, first_row):
        shape = (MARGIN, MARGIN)
        row_at, col_at = infos[0, p], infos[1, p]
        coefs = weights(row_at, col_at, infos[2, p], tile_at)
        shift = iota(shape, 1) - iota(shape, 0) + (first_held - first_row)
        return loc, at, MARGIN, coefs, pick_cols(col_at), ones(shift == row_at)

    def keep(ref, got):
        ref[0] = got[:, :patch]
        ref[1] = got[:, patch:]

    order = list(range(1, n))
    copies_a, copies_b = {}, {}
    local[0].wait()
    for k, got in zip(order, blocks_of([block_job(k) for k in order])):
        keep(block.at[k], got)
        copies_a[k] = remote(
            block.at[k, :, pl.ds(MARGIN, middle), :],
            recv_a.at[k - 1],
            a_send.at[k - 1],
            a_recv.at[k - 1],
            {"beam": lax.rem(me + k, n)},
        )
        copies_a[k].start()

    @pl.when(has_down)
    def _():
        up[0].wait_recv()

    @pl.when(has_up)
    def _():
        down[0].wait_recv()

    spots = [(0, p) for p in range(n)] + [(1, p) for p in range(n)]
    jobs = [edge_job(p, rows - MARGIN, from_below, tile + 1, 0, 0) for p in range(n)]
    jobs += [edge_job(p, 0, from_above, tile - 1, rows + MARGIN, patch - MARGIN) for p in range(n)]
    for (slot, p), got in zip(spots, blocks_of(jobs)):
        keep(edge.at[slot, p], got)

    @pl.when(has_down)
    def _():
        down[2].start()

    @pl.when(has_up)
    def _():
        up[2].start()

    keep(block.at[0], blocks_of([block_job(0)])[0])
    local[1].wait()

    @pl.when(has_down)
    def _():
        up[1].wait_recv()
        up[2].wait_recv()

    @pl.when(has_up)
    def _():
        down[1].wait_recv()
        down[2].wait_recv()

    for k in order + [0]:
        p = lax.rem(me + k, n)
        for c in range(2):
            send_b[k, c, :MARGIN, :] = block[k, c, :MARGIN, :] + halo[0, p, c]
            send_b[k, c, MARGIN:, :] = block[k, c, MARGIN + middle :, :] + halo[1, p, c]
        if k != 0:
            copies_b[k] = remote(
                send_b.at[k], recv_b.at[k - 1], b_send.at[k - 1], b_recv.at[k - 1], {"beam": p}
            )
            copies_b[k].start()

    tall = jnp.concatenate([ploc[...], phalo[...]], 0)
    high, low = split(tall)
    least = (tall - high.astype(jnp.float32) - low.astype(jnp.float32)).astype(jnp.bfloat16)
    row_pick = jnp.concatenate([pick_rows(row_ref[me]), pick_halo(row_ref[me])], 1)
    own_cols = pick_cols(col_ref[me])
    here = None
    for term in (least, low, high):
        now = dot(row_pick, dot(term, own_cols).astype(jnp.bfloat16))
        here = now if here is None else here + now
    here = here * SIGMA_SCALE
    trans[0] = jnp.cos(here)
    trans[1] = jnp.sin(here)

    for k in order:
        copies_a[k].wait_recv()
        copies_b[k].wait_recv()
    local[2].wait()

    parts = []
    for c in range(2):
        mid = block[0, c, MARGIN : MARGIN + middle, :]
        head = send_b[0, c, :MARGIN, :]
        tail = send_b[0, c, MARGIN:, :]
        for k in order:
            mid += recv_a[k - 1, c]
            head += recv_b[k - 1, c, :MARGIN, :]
            tail += recv_b[k - 1, c, MARGIN:, :]
        parts.append(jnp.concatenate([head, mid, tail], 0))
    wave_re, wave_im = parts
    exit_re = trans[0] * wave_re - trans[1] * wave_im
    exit_im = trans[0] * wave_im + trans[1] * wave_re
    ahead = (high_ref[0], low_ref[0])
    back = (high_ref[1], low_ref[1])
    far = transform(jnp.concatenate([exit_re, exit_im], 0), back, ahead)
    far_re, far_im = far[:, :patch], far[:, patch:]
    misfit = far_re * far_re + far_im * far_im - seen[...]
    misfit_ref[...] = misfit
    turned = transform(jnp.concatenate([misfit * far_re, misfit * far_im], 0), ahead, back)
    piece[...] = SIGMA_SCALE * (exit_re * turned[:, patch:] - exit_im * turned[:, :patch])

    copies_p = {}
    for k in order:
        copies_p[k] = remote(
            piece, recv_p.at[k - 1], p_send.at[k - 1], p_recv.at[k - 1], {"beam": lax.rem(me + k, n)}
        )
        copies_p[k].start()

    def place(value, p):
        shape = (patch, cols)
        col_place = ones(iota(shape, 1) - iota(shape, 0) == col_ref[p])
        shape = (rows + 2 * MARGIN, patch)
        row_place = ones(iota(shape, 0) - iota(shape, 1) == row_ref[p])
        moved = dot(jnp.concatenate(split(value), 0), col_place).astype(jnp.bfloat16)
        return dot(jnp.concatenate([row_place, row_place], 1), moved)

    strip[...] = place(piece[...], me)
    for k in order:
        copies_p[k].wait_recv()
        strip[...] += place(recv_p[k - 1], lax.rem(me + n - k, n))

    rim_up = remote(strip.at[first, :], rims.at[1], rim_send.at[0], rim_recv.at[0], {"tile": tile - 1})
    rim_down = remote(strip.at[below, :], rims.at[0], rim_send.at[1], rim_recv.at[1], {"tile": tile + 1})

    @pl.when(has_up)
    def _():
        rim_up.start()

    @pl.when(has_down)
    def _():
        rim_down.start()

    grad_ref[...] = strip[MARGIN : MARGIN + rows, :]

    @pl.when(has_down)
    def _():
        rim_up.wait_recv()
        grad_ref[rows - MARGIN :, :] += rims[1]

    @pl.when(has_up)
    def _():
        rim_down.wait_recv()
        grad_ref[:MARGIN, :] += rims[0]

    for k in order:
        copies_a[k].wait_send()
        copies_b[k].wait_send()
        copies_p[k].wait_send()

    @pl.when(has_up)
    def _():
        for copy in up + [rim_up]:
            copy.wait_send()

    @pl.when(has_down)
    def _():
        for copy in down + [rim_down]:
            copy.wait_send()


def shards(
    n,
    tiles,
    scattering,
    potential,
    row_offset,
    col_offset,
    table_index,
    beam_tilt,
    coef_table,
    measured,
):
    beams, _, rows, cols = scattering.shape
    positions, patch = measured.shape[0], measured.shape[-1]
    assert positions == n and patch & (patch - 1) == 0 and cols & (cols - 1) == 0
    high, low, trig = tables(patch)
    f32 = jnp.float32
    middle = patch - 2 * MARGIN
    smem = pl.BlockSpec(memory_space=pltpu.SMEM)
    vmem = pl.BlockSpec(memory_space=pltpu.VMEM)
    anywhere = pl.BlockSpec(memory_space=pl.ANY)
    strip_rows = rows + 2 * MARGIN
    dma = pltpu.SemaphoreType.DMA
    misfit, grad = pl.pallas_call(
        functools.partial(kernel, n, tiles),
        out_shape=(
            jax.ShapeDtypeStruct((patch, patch), f32),
            jax.ShapeDtypeStruct((rows, cols), f32),
        ),
        in_specs=[smem] * 6 + [vmem] * 2 + [anywhere] * 3,
        out_specs=(vmem, vmem),
        scratch_shapes=[
            pltpu.VMEM((beams, 2, rows, cols), f32),
            pltpu.VMEM((rows, cols), f32),
            pltpu.SMEM((3, n), jnp.int32),
            pltpu.SMEM((3, n), jnp.int32),
            pltpu.SMEM((3, n), jnp.int32),
            pltpu.VMEM((2, n, 2, MARGIN, patch), f32),
            pltpu.VMEM((2, n, 2, MARGIN, patch), f32),
            pltpu.VMEM((2 * MARGIN, cols), f32),
            pltpu.VMEM((patch, patch), f32),
            pltpu.VMEM((n, 2, patch, patch), f32),
            pltpu.VMEM((n, 2, 2 * MARGIN, patch), f32),
            pltpu.VMEM((n - 1, 2, middle, patch), f32),
            pltpu.VMEM((n - 1, 2, 2 * MARGIN, patch), f32),
            pltpu.VMEM((2, patch, patch), f32),
            pltpu.VMEM((patch, patch), f32),
            pltpu.VMEM((n - 1, patch, patch), f32),
            pltpu.VMEM((strip_rows, cols), f32),
            pltpu.VMEM((2, MARGIN, cols), f32),
            dma((3,)),
            dma((6,)),
            dma((6,)),
            dma((n - 1,)),
            dma((n - 1,)),
            dma((n - 1,)),
            dma((n - 1,)),
            dma((n - 1,)),
            dma((n - 1,)),
            dma((2,)),
            dma((2,)),
        ],
        compiler_params=pltpu.CompilerParams(
            collective_id=0, has_side_effects=True, vmem_limit_bytes=56 * 1024 * 1024
        ),
    )(
        row_offset[:, 0],
        col_offset[:, 0],
        table_index[:, 0],
        beam_tilt,
        coef_table.reshape(-1, beams),
        trig,
        high,
        low,
        scattering,
        potential,
        measured,
    )
    return misfit[None, None], grad


def solution(mesh):
    in_specs = (
        P("beam", None, "tile", None),
        P("tile", None),
        P(None, "tile"),
        P(None, "tile"),
        P(None, "tile"),
        P(None, "beam"),
        P(None, None, "beam"),
        P(None, "tile", None, None),
    )
    out_specs = (P("beam", "tile", None, None), P("tile", None))
    run = functools.partial(shards, mesh.shape["beam"], mesh.shape["tile"])
    return jax.shard_map(run, mesh=mesh, in_specs=in_specs, out_specs=out_specs, check_vma=False)
```

```python
import functools
import math

import jax
import jax.numpy as jnp
import numpy as np
from jax import lax
from jax.experimental import pallas as pl
from jax.experimental.pallas import tpu as pltpu
from jax.sharding import PartitionSpec as P

MARGIN = 32
SIGMA_SCALE = 1.0
MESH = pl.DeviceIdType.MESH


def tables(length):
    index = np.arange(length)
    angle = (index[:, None] * index[None, :] % length) * (2.0 * math.pi / length)
    re = np.cos(angle) / math.sqrt(length)
    im = -np.sin(angle) / math.sqrt(length)
    ahead = np.block([[re, im], [-im, re]]).astype(np.float32)
    back = np.block([[re, -im], [im, re]]).astype(np.float32)
    both = np.stack([ahead, back])
    high = both.astype(jnp.bfloat16)
    low = (both - high.astype(np.float32)).astype(jnp.bfloat16)
    turns = np.arange(length) * (2.0 * math.pi / length)
    trig = np.stack([np.cos(turns), np.sin(turns)]).astype(np.float32)
    return high, low, trig


def split(value):
    high = value.astype(jnp.bfloat16)
    low = (value - high.astype(jnp.float32)).astype(jnp.bfloat16)
    return high, low


def dot(left, right):
    return jnp.dot(left, right, preferred_element_type=jnp.float32)


def split_dot(left, right):
    return dot(left[0], right[0]) + (dot(left[0], right[1]) + dot(left[1], right[0]))


def transform(stacked, left_table, right_table):
    length = stacked.shape[-1]
    half = split_dot(left_table, split(stacked))
    wide = jnp.concatenate([half[:length], half[length:]], 1)
    return split_dot(split(wide), right_table)


def kernel(
    n,
    tiles,
    row_ref,
    col_ref,
    index_ref,
    tilt_ref,
    coef_ref,
    trig_ref,
    high_ref,
    low_ref,
    scat,
    pot,
    meas,
    misfit_ref,
    grad_ref,
    loc,
    ploc,
    halo,
    phalo,
    seen,
    block,
    send_b,
    recv_a,
    recv_b,
    trans,
    piece,
    recv_p,
    strip,
    rims,
    local_sem,
    halo_send,
    halo_recv,
    a_send,
    a_recv,
    b_send,
    b_recv,
    p_send,
    p_recv,
    rim_send,
    rim_recv,
):
    me = lax.axis_index("beam")
    tile = lax.axis_index("tile")
    beams = scat.shape[0]
    rows, cols = scat.shape[2], scat.shape[3]
    patch = seen.shape[-1]
    early = patch - MARGIN

    local = [
        pltpu.make_async_copy(scat, loc, local_sem.at[0]),
        pltpu.make_async_copy(pot, ploc, local_sem.at[1]),
        pltpu.make_async_copy(meas.at[me, 0], seen, local_sem.at[2]),
    ]
    for copy in local:
        copy.start()

    barrier = pltpu.get_barrier_semaphore()
    for k in range(1, n):
        pl.semaphore_signal(
            barrier, inc=1, device_id={"beam": lax.rem(me + k, n)}, device_id_type=MESH
        )
    has_up = tile > 0
    has_down = tile < tiles - 1

    @pl.when(has_up)
    def _():
        pl.semaphore_signal(barrier, inc=1, device_id={"tile": tile - 1}, device_id_type=MESH)

    @pl.when(has_down)
    def _():
        pl.semaphore_signal(barrier, inc=1, device_id={"tile": tile + 1}, device_id_type=MESH)

    pl.semaphore_wait(barrier, n - 1 + has_up.astype(jnp.int32) + has_down.astype(jnp.int32))

    def remote(src, dst, send_sem, recv_sem, where):
        return pltpu.make_async_remote_copy(
            src_ref=src,
            dst_ref=dst,
            send_sem=send_sem,
            recv_sem=recv_sem,
            device_id=where,
            device_id_type=MESH,
        )

    last = pl.ds(rows - MARGIN, MARGIN)
    first = pl.ds(0, MARGIN)
    second = pl.ds(MARGIN, MARGIN)
    below = pl.ds(rows + MARGIN, MARGIN)
    up = [
        remote(scat.at[:, :, first, :], halo.at[:, :, second, :], halo_send.at[0], halo_recv.at[0], {"tile": tile - 1}),
        remote(pot.at[first, :], phalo.at[second, :], halo_send.at[1], halo_recv.at[1], {"tile": tile - 1}),
    ]
    down = [
        remote(scat.at[:, :, last, :], halo.at[:, :, first, :], halo_send.at[2], halo_recv.at[2], {"tile": tile + 1}),
        remote(pot.at[last, :], phalo.at[first, :], halo_send.at[3], halo_recv.at[3], {"tile": tile + 1}),
    ]

    @pl.when(has_up)
    def _():
        for copy in up:
            copy.start()

    @pl.when(has_down)
    def _():
        for copy in down:
            copy.start()

    @pl.when(tile == 0)
    def _():
        halo[:, :, :MARGIN, :] = jnp.zeros((beams, 2, MARGIN, cols), jnp.float32)
        phalo[:MARGIN, :] = jnp.zeros((MARGIN, cols), jnp.float32)

    @pl.when(tile == tiles - 1)
    def _():
        halo[:, :, MARGIN:, :] = jnp.zeros((beams, 2, MARGIN, cols), jnp.float32)
        phalo[MARGIN:, :] = jnp.zeros((MARGIN, cols), jnp.float32)

    def weights(p):
        corner = row_ref[p] + tile * rows - MARGIN
        picked = index_ref[p]
        result = []
        for b in range(beams):
            turn = (tilt_ref[0, b] * corner + tilt_ref[1, b] * col_ref[p]) & (patch - 1)
            cos, sin = trig_ref[0, turn], trig_ref[1, turn]
            q_re = coef_ref[picked, b]
            q_im = coef_ref[picked + coef_ref.shape[0] // 2, b]
            result.append((q_re * cos + q_im * sin, q_im * cos - q_re * sin))
        return result

    def iota(shape, axis):
        return lax.broadcasted_iota(jnp.int32, shape, axis)

    def ones(mask):
        return jnp.where(mask, 1.0, 0.0).astype(jnp.bfloat16)

    def pick_cols(p):
        shape = (cols, patch)
        return ones(iota(shape, 0) - iota(shape, 1) == col_ref[p])

    def turn_of(p, shape):
        return jnp.where(jnp.full(shape, row_ref[p], jnp.int32) < MARGIN, MARGIN, 0)

    def pick_rows(p):
        shape = (patch, rows)
        wanted = (iota(shape, 0) + turn_of(p, shape)) & (patch - 1)
        return ones(iota(shape, 1) - wanted == row_ref[p] - MARGIN)

    def pick_halo(p, first_row):
        shape = (patch - first_row, 2 * MARGIN)
        held = iota(shape, 1)
        held = jnp.where(held < MARGIN, held, held + rows)
        wanted = (iota(shape, 0) + first_row + turn_of(p, shape)) & (patch - 1)
        return ones(held - wanted == row_ref[p])

    def unturn(value, p):
        turned = jnp.concatenate([value[early:], value[:early]], 0)
        return jnp.where(turn_of(p, value.shape) > 0, turned, value)

    def combine(source, count, coefs):
        total_re = total_im = None
        for b in range(beams):
            re = source[b, 0, :count, :]
            im = source[b, 1, :count, :]
            c_re, c_im = coefs[b]
            now_re = c_re * re - c_im * im
            now_im = c_re * im + c_im * re
            total_re = now_re if total_re is None else total_re + now_re
            total_im = now_im if total_im is None else total_im + now_im
        return jnp.concatenate(split(total_re) + split(total_im), 0)

    def block_of(combined, col_pick, row_pick):
        count = combined.shape[0] // 4
        chosen = dot(combined, col_pick).astype(jnp.bfloat16)
        chosen = jnp.concatenate([chosen[: 2 * count], chosen[2 * count :]], 1)
        return dot(jnp.concatenate([row_pick, row_pick], 1), chosen)

    order = list(range(1, n))
    coefs = {}
    col_picks = {}
    copies_a, copies_b = {}, {}
    local[0].wait()
    for k in order + [0]:
        p = lax.rem(me + k, n)
        coefs[k] = weights(p)
        col_picks[k] = pick_cols(p)
        got = block_of(combine(loc, rows, coefs[k]), col_picks[k], pick_rows(p))
        block[k, 0] = got[:, :patch]
        block[k, 1] = got[:, patch:]
        if k != 0:
            copies_a[k] = remote(
                block.at[k, :, pl.ds(0, early), :],
                recv_a.at[k - 1],
                a_send.at[k - 1],
                a_recv.at[k - 1],
                {"beam": p},
            )
            copies_a[k].start()

    local[1].wait()

    @pl.when(has_down)
    def _():
        for copy in up:
            copy.wait_recv()

    @pl.when(has_up)
    def _():
        for copy in down:
            copy.wait_recv()

    jobs = [(combine(halo, 2 * MARGIN, coefs[k]), pick_halo(lax.rem(me + k, n), early)) for k in order + [0]]
    for k, (combined, row_pick) in zip(order + [0], jobs):
        p = lax.rem(me + k, n)
        got = block_of(combined, col_picks[k], row_pick)
        for c in range(2):
            send_b[k, c] = block[k, c, early:, :] + got[:, c * patch : (c + 1) * patch]
        if k != 0:
            copies_b[k] = remote(
                send_b.at[k], recv_b.at[k - 1], b_send.at[k - 1], b_recv.at[k - 1], {"beam": p}
            )
            copies_b[k].start()

    tall = jnp.concatenate([ploc[...], phalo[...]], 0)
    high, low = split(tall)
    least = (tall - high.astype(jnp.float32) - low.astype(jnp.float32)).astype(jnp.bfloat16)
    row_pick = jnp.concatenate([pick_rows(me), pick_halo(me, 0)], 1)
    here = None
    for term in (least, low, high):
        now = dot(row_pick, dot(term, col_picks[0]).astype(jnp.bfloat16))
        here = now if here is None else here + now
    here = unturn(here, me) * SIGMA_SCALE
    trans[0] = jnp.cos(here)
    trans[1] = jnp.sin(here)

    for k in order:
        copies_a[k].wait_recv()
        copies_b[k].wait_recv()
    local[2].wait()

    parts = []
    for c in range(2):
        body = block[0, c, :early, :]
        rest = send_b[0, c]
        for k in order:
            body += recv_a[k - 1, c]
            rest += recv_b[k - 1, c]
        parts.append(unturn(jnp.concatenate([body, rest], 0), me))
    wave_re, wave_im = parts
    exit_re = trans[0] * wave_re - trans[1] * wave_im
    exit_im = trans[0] * wave_im + trans[1] * wave_re
    ahead = (high_ref[0], low_ref[0])
    back = (high_ref[1], low_ref[1])
    far = transform(jnp.concatenate([exit_re, exit_im], 0), back, ahead)
    far_re, far_im = far[:, :patch], far[:, patch:]
    misfit = far_re * far_re + far_im * far_im - seen[...]
    misfit_ref[...] = misfit
    turned = transform(jnp.concatenate([misfit * far_re, misfit * far_im], 0), ahead, back)
    piece[...] = SIGMA_SCALE * (exit_re * turned[:, patch:] - exit_im * turned[:, :patch])

    copies_p = {}
    for k in order:
        copies_p[k] = remote(
            piece, recv_p.at[k - 1], p_send.at[k - 1], p_recv.at[k - 1], {"beam": lax.rem(me + k, n)}
        )
        copies_p[k].start()

    def spots(p):
        shape = (patch, cols)
        col_place = ones(iota(shape, 1) - iota(shape, 0) == col_ref[p])
        shape = (rows + 2 * MARGIN, patch)
        row_place = ones(iota(shape, 0) - iota(shape, 1) == row_ref[p])
        return col_place, jnp.concatenate([row_place, row_place], 1)

    def place(value, spot):
        moved = dot(jnp.concatenate(split(value), 0), spot[0]).astype(jnp.bfloat16)
        return dot(spot[1], moved)

    places = [spots(lax.rem(me + n - k, n)) for k in range(n)]
    strip[...] = place(piece[...], places[0])
    for k in order:
        copies_p[k].wait_recv()
        strip[...] += place(recv_p[k - 1], places[k])

    rim_up = remote(strip.at[first, :], rims.at[1], rim_send.at[0], rim_recv.at[0], {"tile": tile - 1})
    rim_down = remote(strip.at[below, :], rims.at[0], rim_send.at[1], rim_recv.at[1], {"tile": tile + 1})

    @pl.when(has_up)
    def _():
        rim_up.start()

    @pl.when(has_down)
    def _():
        rim_down.start()

    grad_ref[...] = strip[MARGIN : MARGIN + rows, :]

    @pl.when(has_down)
    def _():
        rim_up.wait_recv()
        grad_ref[rows - MARGIN :, :] += rims[1]

    @pl.when(has_up)
    def _():
        rim_down.wait_recv()
        grad_ref[:MARGIN, :] += rims[0]

    for k in order:
        copies_a[k].wait_send()
        copies_b[k].wait_send()
        copies_p[k].wait_send()

    @pl.when(has_up)
    def _():
        for copy in up + [rim_up]:
            copy.wait_send()

    @pl.when(has_down)
    def _():
        for copy in down + [rim_down]:
            copy.wait_send()


def shards(
    n,
    tiles,
    scattering,
    potential,
    row_offset,
    col_offset,
    table_index,
    beam_tilt,
    coef_table,
    measured,
):
    beams, _, rows, cols = scattering.shape
    positions, patch = measured.shape[0], measured.shape[-1]
    assert positions == n and patch & (patch - 1) == 0 and cols & (cols - 1) == 0
    high, low, trig = tables(patch)
    f32 = jnp.float32
    early = patch - MARGIN
    smem = pl.BlockSpec(memory_space=pltpu.SMEM)
    vmem = pl.BlockSpec(memory_space=pltpu.VMEM)
    anywhere = pl.BlockSpec(memory_space=pl.ANY)
    strip_rows = rows + 2 * MARGIN
    dma = pltpu.SemaphoreType.DMA
    misfit, grad = pl.pallas_call(
        functools.partial(kernel, n, tiles),
        out_shape=(
            jax.ShapeDtypeStruct((patch, patch), f32),
            jax.ShapeDtypeStruct((rows, cols), f32),
        ),
        in_specs=[smem] * 6 + [vmem] * 2 + [anywhere] * 3,
        out_specs=(vmem, vmem),
        scratch_shapes=[
            pltpu.VMEM((beams, 2, rows, cols), f32),
            pltpu.VMEM((rows, cols), f32),
            pltpu.VMEM((beams, 2, 2 * MARGIN, cols), f32),
            pltpu.VMEM((2 * MARGIN, cols), f32),
            pltpu.VMEM((patch, patch), f32),
            pltpu.VMEM((n, 2, patch, patch), f32),
            pltpu.VMEM((n, 2, MARGIN, patch), f32),
            pltpu.VMEM((n - 1, 2, patch - MARGIN, patch), f32),
            pltpu.VMEM((n - 1, 2, MARGIN, patch), f32),
            pltpu.VMEM((2, patch, patch), f32),
            pltpu.VMEM((patch, patch), f32),
            pltpu.VMEM((n - 1, patch, patch), f32),
            pltpu.VMEM((strip_rows, cols), f32),
            pltpu.VMEM((2, MARGIN, cols), f32),
            dma((3,)),
            dma((4,)),
            dma((4,)),
            dma((n - 1,)),
            dma((n - 1,)),
            dma((n - 1,)),
            dma((n - 1,)),
            dma((n - 1,)),
            dma((n - 1,)),
            dma((2,)),
            dma((2,)),
        ],
        compiler_params=pltpu.CompilerParams(
            collective_id=0, has_side_effects=True, vmem_limit_bytes=56 * 1024 * 1024
        ),
    )(
        row_offset[:, 0],
        col_offset[:, 0],
        table_index[:, 0],
        beam_tilt,
        coef_table.reshape(-1, beams),
        trig,
        high,
        low,
        scattering,
        potential,
        measured,
    )
    return misfit[None, None], grad


def solution(mesh):
    in_specs = (
        P("beam", None, "tile", None),
        P("tile", None),
        P(None, "tile"),
        P(None, "tile"),
        P(None, "tile"),
        P(None, "beam"),
        P(None, None, "beam"),
        P(None, "tile", None, None),
    )
    out_specs = (P("beam", "tile", None, None), P("tile", None))
    run = functools.partial(shards, mesh.shape["beam"], mesh.shape["tile"])
    return jax.shard_map(run, mesh=mesh, in_specs=in_specs, out_specs=out_specs, check_vma=False)
```

```python
import functools
import math

import jax
import jax.numpy as jnp
import numpy as np
from jax import lax
from jax.experimental import pallas as pl
from jax.experimental.pallas import tpu as pltpu
from jax.sharding import PartitionSpec as P

MARGIN = 32
SIGMA_SCALE = 1.0
MESH = pl.DeviceIdType.MESH


def tables(length):
    index = np.arange(length)
    angle = (index[:, None] * index[None, :] % length) * (2.0 * math.pi / length)
    re = np.cos(angle) / math.sqrt(length)
    im = -np.sin(angle) / math.sqrt(length)
    ahead = np.block([[re, im], [-im, re]]).astype(np.float32)
    back = np.block([[re, -im], [im, re]]).astype(np.float32)
    both = np.stack([ahead, back])
    high = both.astype(jnp.bfloat16)
    low = (both - high.astype(np.float32)).astype(jnp.bfloat16)
    turns = np.arange(length) * (2.0 * math.pi / length)
    trig = np.stack([np.cos(turns), np.sin(turns)]).astype(np.float32)
    return high, low, trig


def split(value):
    high = value.astype(jnp.bfloat16)
    low = (value - high.astype(jnp.float32)).astype(jnp.bfloat16)
    return high, low


def dot(left, right):
    return jnp.dot(left, right, preferred_element_type=jnp.float32)


def split_dot(left, right):
    return dot(left[0], right[0]) + (dot(left[0], right[1]) + dot(left[1], right[0]))


def transform(stacked, left_table, right_table):
    length = stacked.shape[-1]
    half = split_dot(left_table, split(stacked))
    wide = jnp.concatenate([half[:length], half[length:]], 1)
    return split_dot(split(wide), right_table)


def kernel(
    n,
    tiles,
    row_ref,
    col_ref,
    index_ref,
    tilt_ref,
    coef_ref,
    trig_ref,
    high_ref,
    low_ref,
    scat,
    pot,
    meas,
    misfit_ref,
    grad_ref,
    loc,
    ploc,
    halo,
    phalo,
    seen,
    block,
    send_b,
    recv_a,
    recv_b,
    trans,
    piece,
    recv_p,
    strip,
    rims,
    local_sem,
    halo_send,
    halo_recv,
    a_send,
    a_recv,
    b_send,
    b_recv,
    p_send,
    p_recv,
    rim_send,
    rim_recv,
):
    me = lax.axis_index("beam")
    tile = lax.axis_index("tile")
    beams = scat.shape[0]
    rows, cols = scat.shape[2], scat.shape[3]
    patch = seen.shape[-1]
    early = patch - MARGIN

    local = [
        pltpu.make_async_copy(scat, loc, local_sem.at[0]),
        pltpu.make_async_copy(pot, ploc, local_sem.at[1]),
        pltpu.make_async_copy(meas.at[me, 0], seen, local_sem.at[2]),
    ]
    for copy in local:
        copy.start()

    barrier = pltpu.get_barrier_semaphore()
    for k in range(1, n):
        pl.semaphore_signal(
            barrier, inc=1, device_id={"beam": lax.rem(me + k, n)}, device_id_type=MESH
        )
    has_up = tile > 0
    has_down = tile < tiles - 1

    @pl.when(has_up)
    def _():
        pl.semaphore_signal(barrier, inc=1, device_id={"tile": tile - 1}, device_id_type=MESH)

    @pl.when(has_down)
    def _():
        pl.semaphore_signal(barrier, inc=1, device_id={"tile": tile + 1}, device_id_type=MESH)

    def weights(p):
        corner = row_ref[p] + tile * rows - MARGIN
        picked = index_ref[p]
        result = []
        for b in range(beams):
            turn = (tilt_ref[0, b] * corner + tilt_ref[1, b] * col_ref[p]) & (patch - 1)
            cos, sin = trig_ref[0, turn], trig_ref[1, turn]
            q_re = coef_ref[picked, b]
            q_im = coef_ref[picked + coef_ref.shape[0] // 2, b]
            result.append((q_re * cos + q_im * sin, q_im * cos - q_re * sin))
        return result

    def iota(shape, axis):
        return lax.broadcasted_iota(jnp.int32, shape, axis)

    def ones(mask):
        return jnp.where(mask, 1.0, 0.0).astype(jnp.bfloat16)

    def pick_cols(p):
        shape = (cols, patch)
        return ones(iota(shape, 0) - iota(shape, 1) == col_ref[p])

    def turn_of(p, shape):
        return jnp.where(jnp.full(shape, row_ref[p], jnp.int32) < MARGIN, MARGIN, 0)

    def pick_rows(p):
        shape = (patch, rows)
        wanted = (iota(shape, 0) + turn_of(p, shape)) & (patch - 1)
        return ones(iota(shape, 1) - wanted == row_ref[p] - MARGIN)

    def pick_halo(p, first_row):
        shape = (patch - first_row, 2 * MARGIN)
        held = iota(shape, 1)
        held = jnp.where(held < MARGIN, held, held + rows)
        wanted = (iota(shape, 0) + first_row + turn_of(p, shape)) & (patch - 1)
        return ones(held - wanted == row_ref[p])

    def unturn(value, p):
        turned = jnp.concatenate([value[early:], value[:early]], 0)
        return jnp.where(turn_of(p, value.shape) > 0, turned, value)

    def combine(source, count, coefs):
        total_re = total_im = None
        for b in range(beams):
            re = source[b, 0, :count, :]
            im = source[b, 1, :count, :]
            c_re, c_im = coefs[b]
            now_re = c_re * re - c_im * im
            now_im = c_re * im + c_im * re
            total_re = now_re if total_re is None else total_re + now_re
            total_im = now_im if total_im is None else total_im + now_im
        return jnp.concatenate(split(total_re) + split(total_im), 0)

    def block_of(combined, col_pick, row_pick):
        count = combined.shape[0] // 4
        chosen = dot(combined, col_pick).astype(jnp.bfloat16)
        chosen = jnp.concatenate([chosen[: 2 * count], chosen[2 * count :]], 1)
        return dot(jnp.concatenate([row_pick, row_pick], 1), chosen)

    order = sorted(range(1, n), key=lambda k: abs(2 * k - n))
    coefs = {}
    col_picks = {}

    def make_block(k):
        p = lax.rem(me + k, n)
        coefs[k] = weights(p)
        col_picks[k] = pick_cols(p)
        got = block_of(combine(loc, rows, coefs[k]), col_picks[k], pick_rows(p))
        block[k, 0] = got[:, :patch]
        block[k, 1] = got[:, patch:]

    local[0].wait()
    make_block(order[0])

    pl.semaphore_wait(barrier, n - 1 + has_up.astype(jnp.int32) + has_down.astype(jnp.int32))

    def remote(src, dst, send_sem, recv_sem, where):
        return pltpu.make_async_remote_copy(
            src_ref=src,
            dst_ref=dst,
            send_sem=send_sem,
            recv_sem=recv_sem,
            device_id=where,
            device_id_type=MESH,
        )

    last = pl.ds(rows - MARGIN, MARGIN)
    first = pl.ds(0, MARGIN)
    second = pl.ds(MARGIN, MARGIN)
    below = pl.ds(rows + MARGIN, MARGIN)
    up = [
        remote(scat.at[:, :, first, :], halo.at[:, :, second, :], halo_send.at[0], halo_recv.at[0], {"tile": tile - 1}),
        remote(pot.at[first, :], phalo.at[second, :], halo_send.at[1], halo_recv.at[1], {"tile": tile - 1}),
    ]
    down = [
        remote(scat.at[:, :, last, :], halo.at[:, :, first, :], halo_send.at[2], halo_recv.at[2], {"tile": tile + 1}),
        remote(pot.at[last, :], phalo.at[first, :], halo_send.at[3], halo_recv.at[3], {"tile": tile + 1}),
    ]

    @pl.when(has_up)
    def _():
        for copy in up:
            copy.start()

    @pl.when(has_down)
    def _():
        for copy in down:
            copy.start()

    @pl.when(tile == 0)
    def _():
        halo[:, :, :MARGIN, :] = jnp.zeros((beams, 2, MARGIN, cols), jnp.float32)
        phalo[:MARGIN, :] = jnp.zeros((MARGIN, cols), jnp.float32)

    @pl.when(tile == tiles - 1)
    def _():
        halo[:, :, MARGIN:, :] = jnp.zeros((beams, 2, MARGIN, cols), jnp.float32)
        phalo[MARGIN:, :] = jnp.zeros((MARGIN, cols), jnp.float32)

    copies_a, copies_b = {}, {}
    for k in order + [0]:
        if k != order[0]:
            make_block(k)
        p = lax.rem(me + k, n)
        if k != 0:
            copies_a[k] = remote(
                block.at[k, :, pl.ds(0, early), :],
                recv_a.at[k - 1],
                a_send.at[k - 1],
                a_recv.at[k - 1],
                {"beam": p},
            )
            copies_a[k].start()

    local[1].wait()

    @pl.when(has_down)
    def _():
        for copy in up:
            copy.wait_recv()

    @pl.when(has_up)
    def _():
        for copy in down:
            copy.wait_recv()

    jobs = [(combine(halo, 2 * MARGIN, coefs[k]), pick_halo(lax.rem(me + k, n), early)) for k in order + [0]]
    for k, (combined, row_pick) in zip(order + [0], jobs):
        p = lax.rem(me + k, n)
        got = block_of(combined, col_picks[k], row_pick)
        for c in range(2):
            send_b[k, c] = block[k, c, early:, :] + got[:, c * patch : (c + 1) * patch]
        if k != 0:
            copies_b[k] = remote(
                send_b.at[k], recv_b.at[k - 1], b_send.at[k - 1], b_recv.at[k - 1], {"beam": p}
            )
            copies_b[k].start()

    tall = jnp.concatenate([ploc[...], phalo[...]], 0)
    high, low = split(tall)
    least = (tall - high.astype(jnp.float32) - low.astype(jnp.float32)).astype(jnp.bfloat16)
    row_pick = jnp.concatenate([pick_rows(me), pick_halo(me, 0)], 1)
    here = None
    for term in (least, low, high):
        now = dot(row_pick, dot(term, col_picks[0]).astype(jnp.bfloat16))
        here = now if here is None else here + now
    here = unturn(here, me) * SIGMA_SCALE
    trans[0] = jnp.cos(here)
    trans[1] = jnp.sin(here)

    for k in order:
        copies_a[k].wait_recv()
        copies_b[k].wait_recv()
    local[2].wait()

    parts = []
    for c in range(2):
        body = block[0, c, :early, :]
        rest = send_b[0, c]
        for k in order:
            body += recv_a[k - 1, c]
            rest += recv_b[k - 1, c]
        parts.append(unturn(jnp.concatenate([body, rest], 0), me))
    wave_re, wave_im = parts
    exit_re = trans[0] * wave_re - trans[1] * wave_im
    exit_im = trans[0] * wave_im + trans[1] * wave_re
    ahead = (high_ref[0], low_ref[0])
    back = (high_ref[1], low_ref[1])
    far = transform(jnp.concatenate([exit_re, exit_im], 0), back, ahead)
    far_re, far_im = far[:, :patch], far[:, patch:]
    misfit = far_re * far_re + far_im * far_im - seen[...]
    misfit_ref[...] = misfit
    turned = transform(jnp.concatenate([misfit * far_re, misfit * far_im], 0), ahead, back)
    piece[...] = SIGMA_SCALE * (exit_re * turned[:, patch:] - exit_im * turned[:, :patch])

    copies_p = {}
    for k in order:
        copies_p[k] = remote(
            piece, recv_p.at[k - 1], p_send.at[k - 1], p_recv.at[k - 1], {"beam": lax.rem(me + k, n)}
        )
        copies_p[k].start()

    def spots(p):
        shape = (patch, cols)
        col_place = ones(iota(shape, 1) - iota(shape, 0) == col_ref[p])
        shape = (rows + 2 * MARGIN, patch)
        row_place = ones(iota(shape, 0) - iota(shape, 1) == row_ref[p])
        return col_place, jnp.concatenate([row_place, row_place], 1)

    def move(value, spot):
        return dot(jnp.concatenate(split(value), 0), spot[0]).astype(jnp.bfloat16)

    places = [spots(lax.rem(me + n - k, n)) for k in range(n)]
    strip[...] = dot(places[0][1], move(piece[...], places[0]))
    for k in order[: n - 3]:
        copies_p[k].wait_recv()
        strip[...] += dot(places[k][1], move(recv_p[k - 1], places[k]))
    final = order[n - 3 :]
    for k in final:
        copies_p[k].wait_recv()
    moved = jnp.concatenate([move(recv_p[k - 1], places[k]) for k in final], 0)
    final_rows = jnp.concatenate([places[k][1] for k in final], 1)
    lower = rows + MARGIN
    rim_rows = jnp.concatenate([final_rows[:MARGIN], final_rows[lower:]], 0)
    rim = dot(rim_rows, moved)
    strip[:MARGIN, :] += rim[:MARGIN]
    strip[lower:, :] += rim[MARGIN:]

    rim_up = remote(strip.at[first, :], rims.at[1], rim_send.at[0], rim_recv.at[0], {"tile": tile - 1})
    rim_down = remote(strip.at[below, :], rims.at[0], rim_send.at[1], rim_recv.at[1], {"tile": tile + 1})

    @pl.when(has_up)
    def _():
        rim_up.start()

    @pl.when(has_down)
    def _():
        rim_down.start()

    grad_ref[...] = strip[MARGIN:lower, :] + dot(final_rows[MARGIN:lower], moved)

    @pl.when(has_down)
    def _():
        rim_up.wait_recv()
        grad_ref[rows - MARGIN :, :] += rims[1]

    @pl.when(has_up)
    def _():
        rim_down.wait_recv()
        grad_ref[:MARGIN, :] += rims[0]

    for k in order:
        copies_a[k].wait_send()
        copies_b[k].wait_send()
        copies_p[k].wait_send()

    @pl.when(has_up)
    def _():
        for copy in up + [rim_up]:
            copy.wait_send()

    @pl.when(has_down)
    def _():
        for copy in down + [rim_down]:
            copy.wait_send()


def shards(
    n,
    tiles,
    scattering,
    potential,
    row_offset,
    col_offset,
    table_index,
    beam_tilt,
    coef_table,
    measured,
):
    beams, _, rows, cols = scattering.shape
    positions, patch = measured.shape[0], measured.shape[-1]
    assert positions == n and patch & (patch - 1) == 0 and cols & (cols - 1) == 0
    high, low, trig = tables(patch)
    f32 = jnp.float32
    early = patch - MARGIN
    smem = pl.BlockSpec(memory_space=pltpu.SMEM)
    vmem = pl.BlockSpec(memory_space=pltpu.VMEM)
    anywhere = pl.BlockSpec(memory_space=pl.ANY)
    strip_rows = rows + 2 * MARGIN
    dma = pltpu.SemaphoreType.DMA
    misfit, grad = pl.pallas_call(
        functools.partial(kernel, n, tiles),
        out_shape=(
            jax.ShapeDtypeStruct((patch, patch), f32),
            jax.ShapeDtypeStruct((rows, cols), f32),
        ),
        in_specs=[smem] * 6 + [vmem] * 2 + [anywhere] * 3,
        out_specs=(vmem, vmem),
        scratch_shapes=[
            pltpu.VMEM((beams, 2, rows, cols), f32),
            pltpu.VMEM((rows, cols), f32),
            pltpu.VMEM((beams, 2, 2 * MARGIN, cols), f32),
            pltpu.VMEM((2 * MARGIN, cols), f32),
            pltpu.VMEM((patch, patch), f32),
            pltpu.VMEM((n, 2, patch, patch), f32),
            pltpu.VMEM((n, 2, MARGIN, patch), f32),
            pltpu.VMEM((n - 1, 2, patch - MARGIN, patch), f32),
            pltpu.VMEM((n - 1, 2, MARGIN, patch), f32),
            pltpu.VMEM((2, patch, patch), f32),
            pltpu.VMEM((patch, patch), f32),
            pltpu.VMEM((n - 1, patch, patch), f32),
            pltpu.VMEM((strip_rows, cols), f32),
            pltpu.VMEM((2, MARGIN, cols), f32),
            dma((3,)),
            dma((4,)),
            dma((4,)),
            dma((n - 1,)),
            dma((n - 1,)),
            dma((n - 1,)),
            dma((n - 1,)),
            dma((n - 1,)),
            dma((n - 1,)),
            dma((2,)),
            dma((2,)),
        ],
        compiler_params=pltpu.CompilerParams(
            collective_id=0, has_side_effects=True, vmem_limit_bytes=56 * 1024 * 1024
        ),
    )(
        row_offset[:, 0],
        col_offset[:, 0],
        table_index[:, 0],
        beam_tilt,
        coef_table.reshape(-1, beams),
        trig,
        high,
        low,
        scattering,
        potential,
        measured,
    )
    return misfit[None, None], grad


def solution(mesh):
    in_specs = (
        P("beam", None, "tile", None),
        P("tile", None),
        P(None, "tile"),
        P(None, "tile"),
        P(None, "tile"),
        P(None, "beam"),
        P(None, None, "beam"),
        P(None, "tile", None, None),
    )
    out_specs = (P("beam", "tile", None, None), P("tile", None))
    run = functools.partial(shards, mesh.shape["beam"], mesh.shape["tile"])
    return jax.shard_map(run, mesh=mesh, in_specs=in_specs, out_specs=out_specs, check_vma=False)
```

```python
import functools
import math

import jax
import jax.numpy as jnp
import numpy as np
from jax import lax
from jax.experimental import pallas as pl
from jax.experimental.pallas import tpu as pltpu
from jax.sharding import PartitionSpec as P

MARGIN = 32
SIGMA_SCALE = 1.0
MESH = pl.DeviceIdType.MESH


def tables(length):
    index = np.arange(length)
    angle = (index[:, None] * index[None, :] % length) * (2.0 * math.pi / length)
    re = np.cos(angle) / math.sqrt(length)
    im = -np.sin(angle) / math.sqrt(length)
    ahead = np.block([[re, im], [-im, re]]).astype(np.float32)
    back = np.block([[re, -im], [im, re]]).astype(np.float32)
    both = np.stack([ahead, back])
    high = both.astype(jnp.bfloat16)
    low = (both - high.astype(np.float32)).astype(jnp.bfloat16)
    turns = np.arange(length) * (2.0 * math.pi / length)
    trig = np.stack([np.cos(turns), np.sin(turns)]).astype(np.float32)
    return high, low, trig


def split(value):
    high = value.astype(jnp.bfloat16)
    low = (value - high.astype(jnp.float32)).astype(jnp.bfloat16)
    return high, low


def dot(left, right):
    return jnp.dot(left, right, preferred_element_type=jnp.float32)


def split_dot(left, right):
    return dot(left[0], right[0]) + (dot(left[0], right[1]) + dot(left[1], right[0]))


def transform(stacked, left_table, right_table):
    length = stacked.shape[-1]
    half = split_dot(left_table, split(stacked))
    wide = jnp.concatenate([half[:length], half[length:]], 1)
    return split_dot(split(wide), right_table)


def kernel(
    n,
    tiles,
    row_ref,
    col_ref,
    index_ref,
    tilt_ref,
    coef_ref,
    trig_ref,
    high_ref,
    low_ref,
    scat,
    pot,
    meas,
    misfit_ref,
    grad_ref,
    halo,
    phalo,
    seen,
    block,
    send_b,
    recv_a,
    recv_b,
    trans,
    piece,
    recv_p,
    strip,
    rims,
    local_sem,
    halo_send,
    halo_recv,
    a_send,
    a_recv,
    b_send,
    b_recv,
    p_send,
    p_recv,
    rim_send,
    rim_recv,
):
    me = lax.axis_index("beam")
    tile = lax.axis_index("tile")
    beams = scat.shape[0]
    rows, cols = scat.shape[2], scat.shape[3]
    patch = seen.shape[-1]
    early = patch - MARGIN

    local = [
        pltpu.make_async_copy(meas.at[me, 0], seen, local_sem.at[0]),
    ]
    for copy in local:
        copy.start()

    barrier = pltpu.get_barrier_semaphore()
    for k in range(1, n):
        pl.semaphore_signal(
            barrier, inc=1, device_id={"beam": lax.rem(me + k, n)}, device_id_type=MESH
        )
    has_up = tile > 0
    has_down = tile < tiles - 1

    @pl.when(has_up)
    def _():
        pl.semaphore_signal(barrier, inc=1, device_id={"tile": tile - 1}, device_id_type=MESH)

    @pl.when(has_down)
    def _():
        pl.semaphore_signal(barrier, inc=1, device_id={"tile": tile + 1}, device_id_type=MESH)

    def weights(p):
        corner = row_ref[p] + tile * rows - MARGIN
        picked = index_ref[p]
        result = []
        for b in range(beams):
            turn = (tilt_ref[0, b] * corner + tilt_ref[1, b] * col_ref[p]) & (patch - 1)
            cos, sin = trig_ref[0, turn], trig_ref[1, turn]
            q_re = coef_ref[picked, b]
            q_im = coef_ref[picked + coef_ref.shape[0] // 2, b]
            result.append((q_re * cos + q_im * sin, q_im * cos - q_re * sin))
        return result

    def iota(shape, axis):
        return lax.broadcasted_iota(jnp.int32, shape, axis)

    def ones(mask):
        return jnp.where(mask, 1.0, 0.0).astype(jnp.bfloat16)

    def pick_cols(p):
        shape = (cols, patch)
        return ones(iota(shape, 0) - iota(shape, 1) == col_ref[p])

    def turn_of(p, shape):
        return jnp.where(jnp.full(shape, row_ref[p], jnp.int32) < MARGIN, MARGIN, 0)

    def pick_rows(p):
        shape = (patch, rows)
        wanted = (iota(shape, 0) + turn_of(p, shape)) & (patch - 1)
        return ones(iota(shape, 1) - wanted == row_ref[p] - MARGIN)

    def pick_halo(p, first_row):
        shape = (patch - first_row, 2 * MARGIN)
        held = iota(shape, 1)
        held = jnp.where(held < MARGIN, held, held + rows)
        wanted = (iota(shape, 0) + first_row + turn_of(p, shape)) & (patch - 1)
        return ones(held - wanted == row_ref[p])

    def unturn(value, p):
        turned = jnp.concatenate([value[early:], value[:early]], 0)
        return jnp.where(turn_of(p, value.shape) > 0, turned, value)

    def combine(source, count, coefs):
        total_re = total_im = None
        for b in range(beams):
            re = source[b, 0, :count, :]
            im = source[b, 1, :count, :]
            c_re, c_im = coefs[b]
            now_re = c_re * re - c_im * im
            now_im = c_re * im + c_im * re
            total_re = now_re if total_re is None else total_re + now_re
            total_im = now_im if total_im is None else total_im + now_im
        return jnp.concatenate(split(total_re) + split(total_im), 0)

    def block_of(combined, col_pick, row_pick):
        count = combined.shape[0] // 4
        chosen = dot(combined, col_pick).astype(jnp.bfloat16)
        chosen = jnp.concatenate([chosen[: 2 * count], chosen[2 * count :]], 1)
        return dot(jnp.concatenate([row_pick, row_pick], 1), chosen)

    order = sorted(range(1, n), key=lambda k: abs(2 * k - n))
    coefs = {}
    col_picks = {}

    def make_block(k):
        p = lax.rem(me + k, n)
        coefs[k] = weights(p)
        col_picks[k] = pick_cols(p)
        got = block_of(combine(scat, rows, coefs[k]), col_picks[k], pick_rows(p))
        block[k, 0] = got[:, :patch]
        block[k, 1] = got[:, patch:]

    make_block(order[0])

    pl.semaphore_wait(barrier, n - 1 + has_up.astype(jnp.int32) + has_down.astype(jnp.int32))

    def remote(src, dst, send_sem, recv_sem, where):
        return pltpu.make_async_remote_copy(
            src_ref=src,
            dst_ref=dst,
            send_sem=send_sem,
            recv_sem=recv_sem,
            device_id=where,
            device_id_type=MESH,
        )

    last = pl.ds(rows - MARGIN, MARGIN)
    first = pl.ds(0, MARGIN)
    second = pl.ds(MARGIN, MARGIN)
    below = pl.ds(rows + MARGIN, MARGIN)
    up = [
        remote(scat.at[:, :, first, :], halo.at[:, :, second, :], halo_send.at[0], halo_recv.at[0], {"tile": tile - 1}),
        remote(pot.at[first, :], phalo.at[second, :], halo_send.at[1], halo_recv.at[1], {"tile": tile - 1}),
    ]
    down = [
        remote(scat.at[:, :, last, :], halo.at[:, :, first, :], halo_send.at[2], halo_recv.at[2], {"tile": tile + 1}),
        remote(pot.at[last, :], phalo.at[first, :], halo_send.at[3], halo_recv.at[3], {"tile": tile + 1}),
    ]

    @pl.when(has_up)
    def _():
        for copy in up:
            copy.start()

    @pl.when(has_down)
    def _():
        for copy in down:
            copy.start()

    @pl.when(tile == 0)
    def _():
        halo[:, :, :MARGIN, :] = jnp.zeros((beams, 2, MARGIN, cols), jnp.float32)
        phalo[:MARGIN, :] = jnp.zeros((MARGIN, cols), jnp.float32)

    @pl.when(tile == tiles - 1)
    def _():
        halo[:, :, MARGIN:, :] = jnp.zeros((beams, 2, MARGIN, cols), jnp.float32)
        phalo[MARGIN:, :] = jnp.zeros((MARGIN, cols), jnp.float32)

    copies_a, copies_b = {}, {}
    for k in order + [0]:
        if k != order[0]:
            make_block(k)
        p = lax.rem(me + k, n)
        if k != 0:
            copies_a[k] = remote(
                block.at[k, :, pl.ds(0, early), :],
                recv_a.at[k - 1],
                a_send.at[k - 1],
                a_recv.at[k - 1],
                {"beam": p},
            )
            copies_a[k].start()


    @pl.when(has_down)
    def _():
        for copy in up:
            copy.wait_recv()

    @pl.when(has_up)
    def _():
        for copy in down:
            copy.wait_recv()

    jobs = [(combine(halo, 2 * MARGIN, coefs[k]), pick_halo(lax.rem(me + k, n), early)) for k in order + [0]]
    for k, (combined, row_pick) in zip(order + [0], jobs):
        p = lax.rem(me + k, n)
        got = block_of(combined, col_picks[k], row_pick)
        for c in range(2):
            send_b[k, c] = block[k, c, early:, :] + got[:, c * patch : (c + 1) * patch]
        if k != 0:
            copies_b[k] = remote(
                send_b.at[k], recv_b.at[k - 1], b_send.at[k - 1], b_recv.at[k - 1], {"beam": p}
            )
            copies_b[k].start()

    tall = jnp.concatenate([pot[...], phalo[...]], 0)
    high, low = split(tall)
    least = (tall - high.astype(jnp.float32) - low.astype(jnp.float32)).astype(jnp.bfloat16)
    row_pick = jnp.concatenate([pick_rows(me), pick_halo(me, 0)], 1)
    here = None
    for term in (least, low, high):
        now = dot(row_pick, dot(term, col_picks[0]).astype(jnp.bfloat16))
        here = now if here is None else here + now
    here = unturn(here, me) * SIGMA_SCALE
    trans[0] = jnp.cos(here)
    trans[1] = jnp.sin(here)

    for k in order:
        copies_a[k].wait_recv()
        copies_b[k].wait_recv()
    local[0].wait()

    parts = []
    for c in range(2):
        body = block[0, c, :early, :]
        rest = send_b[0, c]
        for k in order:
            body += recv_a[k - 1, c]
            rest += recv_b[k - 1, c]
        parts.append(unturn(jnp.concatenate([body, rest], 0), me))
    wave_re, wave_im = parts
    exit_re = trans[0] * wave_re - trans[1] * wave_im
    exit_im = trans[0] * wave_im + trans[1] * wave_re
    ahead = (high_ref[0], low_ref[0])
    back = (high_ref[1], low_ref[1])
    far = transform(jnp.concatenate([exit_re, exit_im], 0), back, ahead)
    far_re, far_im = far[:, :patch], far[:, patch:]
    misfit = far_re * far_re + far_im * far_im - seen[...]
    misfit_ref[...] = misfit
    turned = transform(jnp.concatenate([misfit * far_re, misfit * far_im], 0), ahead, back)
    piece[...] = SIGMA_SCALE * (exit_re * turned[:, patch:] - exit_im * turned[:, :patch])

    copies_p = {}
    for k in order:
        copies_p[k] = remote(
            piece, recv_p.at[k - 1], p_send.at[k - 1], p_recv.at[k - 1], {"beam": lax.rem(me + k, n)}
        )
        copies_p[k].start()

    def spots(p):
        shape = (patch, cols)
        col_place = ones(iota(shape, 1) - iota(shape, 0) == col_ref[p])
        shape = (rows + 2 * MARGIN, patch)
        row_place = ones(iota(shape, 0) - iota(shape, 1) == row_ref[p])
        return col_place, jnp.concatenate([row_place, row_place], 1)

    def move(value, spot):
        return dot(jnp.concatenate(split(value), 0), spot[0]).astype(jnp.bfloat16)

    places = [spots(lax.rem(me + n - k, n)) for k in range(n)]
    strip[...] = dot(places[0][1], move(piece[...], places[0]))
    near, far_k = order[1:], order[0]
    for k in near:
        copies_p[k].wait_recv()
    moved = jnp.concatenate([move(recv_p[k - 1], places[k]) for k in near], 0)
    strip[...] += dot(jnp.concatenate([places[k][1] for k in near], 1), moved)
    copies_p[far_k].wait_recv()
    moved = move(recv_p[far_k - 1], places[far_k])
    final_rows = places[far_k][1]
    lower = rows + MARGIN
    rim_rows = jnp.concatenate([final_rows[:MARGIN], final_rows[lower:]], 0)
    rim = dot(rim_rows, moved)
    strip[:MARGIN, :] += rim[:MARGIN]
    strip[lower:, :] += rim[MARGIN:]

    rim_up = remote(strip.at[first, :], rims.at[1], rim_send.at[0], rim_recv.at[0], {"tile": tile - 1})
    rim_down = remote(strip.at[below, :], rims.at[0], rim_send.at[1], rim_recv.at[1], {"tile": tile + 1})

    @pl.when(has_up)
    def _():
        rim_up.start()

    @pl.when(has_down)
    def _():
        rim_down.start()

    grad_ref[...] = strip[MARGIN:lower, :] + dot(final_rows[MARGIN:lower], moved)

    @pl.when(has_down)
    def _():
        rim_up.wait_recv()
        grad_ref[rows - MARGIN :, :] += rims[1]

    @pl.when(has_up)
    def _():
        rim_down.wait_recv()
        grad_ref[:MARGIN, :] += rims[0]

    for k in order:
        copies_a[k].wait_send()
        copies_b[k].wait_send()
        copies_p[k].wait_send()

    @pl.when(has_up)
    def _():
        for copy in up + [rim_up]:
            copy.wait_send()

    @pl.when(has_down)
    def _():
        for copy in down + [rim_down]:
            copy.wait_send()


def shards(
    n,
    tiles,
    scattering,
    potential,
    row_offset,
    col_offset,
    table_index,
    beam_tilt,
    coef_table,
    measured,
):
    beams, _, rows, cols = scattering.shape
    positions, patch = measured.shape[0], measured.shape[-1]
    assert positions == n and patch & (patch - 1) == 0 and cols & (cols - 1) == 0
    high, low, trig = tables(patch)
    f32 = jnp.float32
    early = patch - MARGIN
    smem = pl.BlockSpec(memory_space=pltpu.SMEM)
    vmem = pl.BlockSpec(memory_space=pltpu.VMEM)
    anywhere = pl.BlockSpec(memory_space=pl.ANY)
    strip_rows = rows + 2 * MARGIN
    dma = pltpu.SemaphoreType.DMA
    misfit, grad = pl.pallas_call(
        functools.partial(kernel, n, tiles),
        out_shape=(
            jax.ShapeDtypeStruct((patch, patch), f32),
            jax.ShapeDtypeStruct((rows, cols), f32),
        ),
        in_specs=[smem] * 6 + [vmem] * 4 + [anywhere],
        out_specs=(vmem, vmem),
        scratch_shapes=[
            pltpu.VMEM((beams, 2, 2 * MARGIN, cols), f32),
            pltpu.VMEM((2 * MARGIN, cols), f32),
            pltpu.VMEM((patch, patch), f32),
            pltpu.VMEM((n, 2, patch, patch), f32),
            pltpu.VMEM((n, 2, MARGIN, patch), f32),
            pltpu.VMEM((n - 1, 2, patch - MARGIN, patch), f32),
            pltpu.VMEM((n - 1, 2, MARGIN, patch), f32),
            pltpu.VMEM((2, patch, patch), f32),
            pltpu.VMEM((patch, patch), f32),
            pltpu.VMEM((n - 1, patch, patch), f32),
            pltpu.VMEM((strip_rows, cols), f32),
            pltpu.VMEM((2, MARGIN, cols), f32),
            dma((1,)),
            dma((4,)),
            dma((4,)),
            dma((n - 1,)),
            dma((n - 1,)),
            dma((n - 1,)),
            dma((n - 1,)),
            dma((n - 1,)),
            dma((n - 1,)),
            dma((2,)),
            dma((2,)),
        ],
        compiler_params=pltpu.CompilerParams(
            collective_id=0, has_side_effects=True, vmem_limit_bytes=12 * 1024 * 1024
        ),
    )(
        row_offset[:, 0],
        col_offset[:, 0],
        table_index[:, 0],
        beam_tilt,
        coef_table.reshape(-1, beams),
        trig,
        high,
        low,
        scattering,
        potential,
        measured,
    )
    return misfit[None, None], grad


def solution(mesh):
    in_specs = (
        P("beam", None, "tile", None),
        P("tile", None),
        P(None, "tile"),
        P(None, "tile"),
        P(None, "tile"),
        P(None, "beam"),
        P(None, None, "beam"),
        P(None, "tile", None, None),
    )
    out_specs = (P("beam", "tile", None, None), P("tile", None))
    run = functools.partial(shards, mesh.shape["beam"], mesh.shape["tile"])
    return jax.shard_map(run, mesh=mesh, in_specs=in_specs, out_specs=out_specs, check_vma=False)
```

```python
import functools
import math

import jax
import jax.numpy as jnp
import numpy as np
from jax import lax
from jax.experimental import pallas as pl
from jax.experimental.pallas import tpu as pltpu
from jax.sharding import PartitionSpec as P

MARGIN = 32
SIGMA_SCALE = 1.0
MESH = pl.DeviceIdType.MESH


def tables(length):
    index = np.arange(length)
    angle = (index[:, None] * index[None, :] % length) * (2.0 * math.pi / length)
    re = np.cos(angle) / math.sqrt(length)
    im = -np.sin(angle) / math.sqrt(length)
    ahead = np.block([[re, im], [-im, re]]).astype(np.float32)
    back = np.block([[re, -im], [im, re]]).astype(np.float32)
    both = np.stack([ahead, back])
    high = both.astype(jnp.bfloat16)
    low = (both - high.astype(np.float32)).astype(jnp.bfloat16)
    turns = np.arange(length) * (2.0 * math.pi / length)
    trig = np.stack([np.cos(turns), np.sin(turns)]).astype(np.float32)
    return high, low, trig


def split(value):
    high = value.astype(jnp.bfloat16)
    low = (value - high.astype(jnp.float32)).astype(jnp.bfloat16)
    return high, low


def dot(left, right):
    return jnp.dot(left, right, preferred_element_type=jnp.float32)


def split_dot(left, right):
    return dot(left[0], right[0]) + (dot(left[0], right[1]) + dot(left[1], right[0]))


def transform(stacked, left_table, right_table):
    length = stacked.shape[-1]
    half = split_dot(left_table, split(stacked))
    wide = jnp.concatenate([half[:length], half[length:]], 1)
    return split_dot(split(wide), right_table)


def kernel(
    n,
    tiles,
    row_in,
    col_in,
    index_in,
    tilt_in,
    coef_in,
    trig_in,
    high_in,
    low_in,
    scat_in,
    pot_in,
    meas,
    misfit_ref,
    grad_ref,
    row_ref,
    col_ref,
    index_ref,
    tilt_ref,
    coef_ref,
    trig_ref,
    high_ref,
    low_ref,
    scat,
    pot,
    halo,
    phalo,
    seen,
    block,
    send_b,
    recv_a,
    recv_b,
    trans,
    piece,
    recv_p,
    strip,
    rims,
    local_sem,
    halo_send,
    halo_recv,
    a_send,
    a_recv,
    b_send,
    b_recv,
    p_send,
    p_recv,
    rim_send,
    rim_recv,
):
    me = lax.axis_index("beam")
    tile = lax.axis_index("tile")
    beams = scat_in.shape[0]
    rows, cols = scat_in.shape[2], scat_in.shape[3]
    patch = seen.shape[-1]
    early = patch - MARGIN

    barrier = pltpu.get_barrier_semaphore()
    for k in range(1, n):
        pl.semaphore_signal(
            barrier, inc=1, device_id={"beam": lax.rem(me + k, n)}, device_id_type=MESH
        )
    has_up = tile > 0
    has_down = tile < tiles - 1

    @pl.when(has_up)
    def _():
        pl.semaphore_signal(barrier, inc=1, device_id={"tile": tile - 1}, device_id_type=MESH)

    @pl.when(has_down)
    def _():
        pl.semaphore_signal(barrier, inc=1, device_id={"tile": tile + 1}, device_id_type=MESH)

    pairs = [
        (scat_in, scat),
        (row_in, row_ref),
        (col_in, col_ref),
        (index_in, index_ref),
        (tilt_in, tilt_ref),
        (coef_in, coef_ref),
        (trig_in, trig_ref),
        (pot_in, pot),
        (meas.at[me, 0], seen),
        (high_in, high_ref),
        (low_in, low_ref),
    ]
    local = [
        pltpu.make_async_copy(src, dst, local_sem.at[i]) for i, (src, dst) in enumerate(pairs)
    ]
    for copy in local:
        copy.start()

    def weights(p):
        corner = row_ref[p] + tile * rows - MARGIN
        picked = index_ref[p]
        result = []
        for b in range(beams):
            turn = (tilt_ref[0, b] * corner + tilt_ref[1, b] * col_ref[p]) & (patch - 1)
            cos, sin = trig_ref[0, turn], trig_ref[1, turn]
            q_re = coef_ref[picked, b]
            q_im = coef_ref[picked + coef_ref.shape[0] // 2, b]
            result.append((q_re * cos + q_im * sin, q_im * cos - q_re * sin))
        return result

    def iota(shape, axis):
        return lax.broadcasted_iota(jnp.int32, shape, axis)

    def ones(mask):
        return jnp.where(mask, 1.0, 0.0).astype(jnp.bfloat16)

    def pick_cols(p):
        shape = (cols, patch)
        return ones(iota(shape, 0) - iota(shape, 1) == col_ref[p])

    def turn_of(p, shape):
        return jnp.where(jnp.full(shape, row_ref[p], jnp.int32) < MARGIN, MARGIN, 0)

    def pick_rows(p):
        shape = (patch, rows)
        wanted = (iota(shape, 0) + turn_of(p, shape)) & (patch - 1)
        return ones(iota(shape, 1) - wanted == row_ref[p] - MARGIN)

    def pick_halo(p, first_row):
        shape = (patch - first_row, 2 * MARGIN)
        held = iota(shape, 1)
        held = jnp.where(held < MARGIN, held, held + rows)
        wanted = (iota(shape, 0) + first_row + turn_of(p, shape)) & (patch - 1)
        return ones(held - wanted == row_ref[p])

    def unturn(value, p):
        turned = jnp.concatenate([value[early:], value[:early]], 0)
        return jnp.where(turn_of(p, value.shape) > 0, turned, value)

    def combine(source, count, coefs):
        total_re = total_im = None
        for b in range(beams):
            re = source[b, 0, :count, :]
            im = source[b, 1, :count, :]
            c_re, c_im = coefs[b]
            now_re = c_re * re - c_im * im
            now_im = c_re * im + c_im * re
            total_re = now_re if total_re is None else total_re + now_re
            total_im = now_im if total_im is None else total_im + now_im
        return jnp.concatenate(split(total_re) + split(total_im), 0)

    def block_of(combined, col_pick, row_pick):
        count = combined.shape[0] // 4
        chosen = dot(combined, col_pick).astype(jnp.bfloat16)
        chosen = jnp.concatenate([chosen[: 2 * count], chosen[2 * count :]], 1)
        return dot(jnp.concatenate([row_pick, row_pick], 1), chosen)

    order = sorted(range(1, n), key=lambda k: abs(2 * k - n))
    coefs = {}
    col_picks = {}

    def make_block(k):
        p = lax.rem(me + k, n)
        coefs[k] = weights(p)
        col_picks[k] = pick_cols(p)
        got = block_of(combine(scat, rows, coefs[k]), col_picks[k], pick_rows(p))
        block[k, 0] = got[:, :patch]
        block[k, 1] = got[:, patch:]

    for copy in local[:7]:
        copy.wait()
    make_block(order[0])

    pl.semaphore_wait(barrier, n - 1 + has_up.astype(jnp.int32) + has_down.astype(jnp.int32))

    def remote(src, dst, send_sem, recv_sem, where):
        return pltpu.make_async_remote_copy(
            src_ref=src,
            dst_ref=dst,
            send_sem=send_sem,
            recv_sem=recv_sem,
            device_id=where,
            device_id_type=MESH,
        )

    last = pl.ds(rows - MARGIN, MARGIN)
    first = pl.ds(0, MARGIN)
    second = pl.ds(MARGIN, MARGIN)
    below = pl.ds(rows + MARGIN, MARGIN)
    up = [
        remote(scat_in.at[:, :, first, :], halo.at[:, :, second, :], halo_send.at[0], halo_recv.at[0], {"tile": tile - 1}),
        remote(pot_in.at[first, :], phalo.at[second, :], halo_send.at[1], halo_recv.at[1], {"tile": tile - 1}),
    ]
    down = [
        remote(scat_in.at[:, :, last, :], halo.at[:, :, first, :], halo_send.at[2], halo_recv.at[2], {"tile": tile + 1}),
        remote(pot_in.at[last, :], phalo.at[first, :], halo_send.at[3], halo_recv.at[3], {"tile": tile + 1}),
    ]

    @pl.when(has_up)
    def _():
        for copy in up:
            copy.start()

    @pl.when(has_down)
    def _():
        for copy in down:
            copy.start()

    @pl.when(tile == 0)
    def _():
        halo[:, :, :MARGIN, :] = jnp.zeros((beams, 2, MARGIN, cols), jnp.float32)
        phalo[:MARGIN, :] = jnp.zeros((MARGIN, cols), jnp.float32)

    @pl.when(tile == tiles - 1)
    def _():
        halo[:, :, MARGIN:, :] = jnp.zeros((beams, 2, MARGIN, cols), jnp.float32)
        phalo[MARGIN:, :] = jnp.zeros((MARGIN, cols), jnp.float32)

    copies_a, copies_b = {}, {}
    for k in order + [0]:
        if k != order[0]:
            make_block(k)
        p = lax.rem(me + k, n)
        if k != 0:
            copies_a[k] = remote(
                block.at[k, :, pl.ds(0, early), :],
                recv_a.at[k - 1],
                a_send.at[k - 1],
                a_recv.at[k - 1],
                {"beam": p},
            )
            copies_a[k].start()


    @pl.when(has_down)
    def _():
        for copy in up:
            copy.wait_recv()

    @pl.when(has_up)
    def _():
        for copy in down:
            copy.wait_recv()

    jobs = [(combine(halo, 2 * MARGIN, coefs[k]), pick_halo(lax.rem(me + k, n), early)) for k in order + [0]]
    for k, (combined, row_pick) in zip(order + [0], jobs):
        p = lax.rem(me + k, n)
        got = block_of(combined, col_picks[k], row_pick)
        for c in range(2):
            send_b[k, c] = block[k, c, early:, :] + got[:, c * patch : (c + 1) * patch]
        if k != 0:
            copies_b[k] = remote(
                send_b.at[k], recv_b.at[k - 1], b_send.at[k - 1], b_recv.at[k - 1], {"beam": p}
            )
            copies_b[k].start()

    local[7].wait()
    tall = jnp.concatenate([pot[...], phalo[...]], 0)
    high, low = split(tall)
    least = (tall - high.astype(jnp.float32) - low.astype(jnp.float32)).astype(jnp.bfloat16)
    row_pick = jnp.concatenate([pick_rows(me), pick_halo(me, 0)], 1)
    here = None
    for term in (least, low, high):
        now = dot(row_pick, dot(term, col_picks[0]).astype(jnp.bfloat16))
        here = now if here is None else here + now
    here = unturn(here, me) * SIGMA_SCALE
    trans[0] = jnp.cos(here)
    trans[1] = jnp.sin(here)

    for k in order:
        copies_a[k].wait_recv()
        copies_b[k].wait_recv()
    for copy in local[8:]:
        copy.wait()

    parts = []
    for c in range(2):
        body = block[0, c, :early, :]
        rest = send_b[0, c]
        for k in order:
            body += recv_a[k - 1, c]
            rest += recv_b[k - 1, c]
        parts.append(unturn(jnp.concatenate([body, rest], 0), me))
    wave_re, wave_im = parts
    exit_re = trans[0] * wave_re - trans[1] * wave_im
    exit_im = trans[0] * wave_im + trans[1] * wave_re
    ahead = (high_ref[0], low_ref[0])
    back = (high_ref[1], low_ref[1])
    far = transform(jnp.concatenate([exit_re, exit_im], 0), back, ahead)
    far_re, far_im = far[:, :patch], far[:, patch:]
    misfit = far_re * far_re + far_im * far_im - seen[...]
    misfit_ref[...] = misfit
    turned = transform(jnp.concatenate([misfit * far_re, misfit * far_im], 0), ahead, back)
    piece[...] = SIGMA_SCALE * (exit_re * turned[:, patch:] - exit_im * turned[:, :patch])

    copies_p = {}
    for k in order:
        copies_p[k] = remote(
            piece, recv_p.at[k - 1], p_send.at[k - 1], p_recv.at[k - 1], {"beam": lax.rem(me + k, n)}
        )
        copies_p[k].start()

    def spots(p):
        shape = (patch, cols)
        col_place = ones(iota(shape, 1) - iota(shape, 0) == col_ref[p])
        shape = (rows + 2 * MARGIN, patch)
        row_place = ones(iota(shape, 0) - iota(shape, 1) == row_ref[p])
        return col_place, jnp.concatenate([row_place, row_place], 1)

    def move(value, spot):
        return dot(jnp.concatenate(split(value), 0), spot[0]).astype(jnp.bfloat16)

    places = [spots(lax.rem(me + n - k, n)) for k in range(n)]
    strip[...] = dot(places[0][1], move(piece[...], places[0]))
    near, far_k = order[1:], order[0]
    for k in near:
        copies_p[k].wait_recv()
    moved = jnp.concatenate([move(recv_p[k - 1], places[k]) for k in near], 0)
    strip[...] += dot(jnp.concatenate([places[k][1] for k in near], 1), moved)
    copies_p[far_k].wait_recv()
    moved = move(recv_p[far_k - 1], places[far_k])
    final_rows = places[far_k][1]
    lower = rows + MARGIN
    rim_rows = jnp.concatenate([final_rows[:MARGIN], final_rows[lower:]], 0)
    rim = dot(rim_rows, moved)
    strip[:MARGIN, :] += rim[:MARGIN]
    strip[lower:, :] += rim[MARGIN:]

    rim_up = remote(strip.at[first, :], rims.at[1], rim_send.at[0], rim_recv.at[0], {"tile": tile - 1})
    rim_down = remote(strip.at[below, :], rims.at[0], rim_send.at[1], rim_recv.at[1], {"tile": tile + 1})

    @pl.when(has_up)
    def _():
        rim_up.start()

    @pl.when(has_down)
    def _():
        rim_down.start()

    grad_ref[...] = strip[MARGIN:lower, :] + dot(final_rows[MARGIN:lower], moved)

    @pl.when(has_down)
    def _():
        rim_up.wait_recv()
        grad_ref[rows - MARGIN :, :] += rims[1]

    @pl.when(has_up)
    def _():
        rim_down.wait_recv()
        grad_ref[:MARGIN, :] += rims[0]

    for k in order:
        copies_a[k].wait_send()
        copies_b[k].wait_send()
        copies_p[k].wait_send()

    @pl.when(has_up)
    def _():
        for copy in up + [rim_up]:
            copy.wait_send()

    @pl.when(has_down)
    def _():
        for copy in down + [rim_down]:
            copy.wait_send()


def shards(
    n,
    tiles,
    scattering,
    potential,
    row_offset,
    col_offset,
    table_index,
    beam_tilt,
    coef_table,
    measured,
):
    beams, _, rows, cols = scattering.shape
    positions, patch = measured.shape[0], measured.shape[-1]
    assert positions == n and patch & (patch - 1) == 0 and cols & (cols - 1) == 0
    high, low, trig = tables(patch)
    coefs = coef_table.reshape(-1, beams)
    f32 = jnp.float32
    early = patch - MARGIN
    i32 = jnp.int32
    vmem = pl.BlockSpec(memory_space=pltpu.VMEM)
    anywhere = pl.BlockSpec(memory_space=pl.ANY)
    strip_rows = rows + 2 * MARGIN
    dma = pltpu.SemaphoreType.DMA
    misfit, grad = pl.pallas_call(
        functools.partial(kernel, n, tiles),
        out_shape=(
            jax.ShapeDtypeStruct((patch, patch), f32),
            jax.ShapeDtypeStruct((rows, cols), f32),
        ),
        in_specs=[anywhere] * 11,
        out_specs=(vmem, vmem),
        scratch_shapes=[
            pltpu.SMEM((n,), i32),
            pltpu.SMEM((n,), i32),
            pltpu.SMEM((n,), i32),
            pltpu.SMEM((2, beams), i32),
            pltpu.SMEM(coefs.shape, f32),
            pltpu.SMEM(trig.shape, f32),
            pltpu.VMEM(high.shape, jnp.bfloat16),
            pltpu.VMEM(low.shape, jnp.bfloat16),
            pltpu.VMEM((beams, 2, rows, cols), f32),
            pltpu.VMEM((rows, cols), f32),
            pltpu.VMEM((beams, 2, 2 * MARGIN, cols), f32),
            pltpu.VMEM((2 * MARGIN, cols), f32),
            pltpu.VMEM((patch, patch), f32),
            pltpu.VMEM((n, 2, patch, patch), f32),
            pltpu.VMEM((n, 2, MARGIN, patch), f32),
            pltpu.VMEM((n - 1, 2, patch - MARGIN, patch), f32),
            pltpu.VMEM((n - 1, 2, MARGIN, patch), f32),
            pltpu.VMEM((2, patch, patch), f32),
            pltpu.VMEM((patch, patch), f32),
            pltpu.VMEM((n - 1, patch, patch), f32),
            pltpu.VMEM((strip_rows, cols), f32),
            pltpu.VMEM((2, MARGIN, cols), f32),
            dma((11,)),
            dma((4,)),
            dma((4,)),
            dma((n - 1,)),
            dma((n - 1,)),
            dma((n - 1,)),
            dma((n - 1,)),
            dma((n - 1,)),
            dma((n - 1,)),
            dma((2,)),
            dma((2,)),
        ],
        compiler_params=pltpu.CompilerParams(
            collective_id=0, has_side_effects=True, vmem_limit_bytes=56 * 1024 * 1024
        ),
    )(
        row_offset[:, 0],
        col_offset[:, 0],
        table_index[:, 0],
        beam_tilt,
        coefs,
        trig,
        high,
        low,
        scattering,
        potential,
        measured,
    )
    return misfit[None, None], grad


def solution(mesh):
    in_specs = (
        P("beam", None, "tile", None),
        P("tile", None),
        P(None, "tile"),
        P(None, "tile"),
        P(None, "tile"),
        P(None, "beam"),
        P(None, None, "beam"),
        P(None, "tile", None, None),
    )
    out_specs = (P("beam", "tile", None, None), P("tile", None))
    run = functools.partial(shards, mesh.shape["beam"], mesh.shape["tile"])
    return jax.shard_map(run, mesh=mesh, in_specs=in_specs, out_specs=out_specs, check_vma=False)
```

```python
import functools
import math

import jax
import jax.numpy as jnp
import numpy as np
from jax import lax
from jax.experimental import pallas as pl
from jax.experimental.pallas import tpu as pltpu
from jax.sharding import PartitionSpec as P

MARGIN = 32
SIGMA_SCALE = 1.0
MESH = pl.DeviceIdType.MESH


def tables(length):
    index = np.arange(length)
    angle = (index[:, None] * index[None, :] % length) * (2.0 * math.pi / length)
    re = np.cos(angle) / math.sqrt(length)
    im = -np.sin(angle) / math.sqrt(length)
    ahead = np.block([[re, im], [-im, re]]).astype(np.float32)
    back = np.block([[re, -im], [im, re]]).astype(np.float32)
    both = np.stack([ahead, back])
    high = both.astype(jnp.bfloat16)
    low = (both - high.astype(np.float32)).astype(jnp.bfloat16)
    turns = np.arange(length) * (2.0 * math.pi / length)
    trig = np.stack([np.cos(turns), np.sin(turns)]).astype(np.float32)
    return high, low, trig


def split(value):
    high = value.astype(jnp.bfloat16)
    low = (value - high.astype(jnp.float32)).astype(jnp.bfloat16)
    return high, low


def dot(left, right):
    return jnp.dot(left, right, preferred_element_type=jnp.float32)


def split_dot(left, right):
    return dot(left[0], right[0]) + (dot(left[0], right[1]) + dot(left[1], right[0]))


def transform(stacked, left_table, right_table):
    length = stacked.shape[-1]
    half = split_dot(left_table, split(stacked))
    wide = jnp.concatenate([half[:length], half[length:]], 1)
    return split_dot(split(wide), right_table)


def kernel(
    n,
    tiles,
    row_in,
    col_in,
    index_in,
    tilt_in,
    coef_in,
    trig_in,
    high_in,
    low_in,
    scat_in,
    pot_in,
    meas,
    misfit_ref,
    grad_ref,
    row_ref,
    col_ref,
    index_ref,
    tilt_ref,
    coef_ref,
    trig_ref,
    high_ref,
    low_ref,
    scat,
    pot,
    halo,
    phalo,
    seen,
    block,
    send_b,
    recv_a,
    recv_b,
    trans,
    piece,
    recv_p,
    strip,
    rims,
    local_sem,
    halo_send,
    halo_recv,
    a_send,
    a_recv,
    b_send,
    b_recv,
    p_send,
    p_recv,
    rim_send,
    rim_recv,
):
    me = lax.axis_index("beam")
    tile = lax.axis_index("tile")
    beams = scat_in.shape[0]
    rows, cols = scat_in.shape[2], scat_in.shape[3]
    patch = seen.shape[-1]
    early = patch - MARGIN

    barrier = pltpu.get_barrier_semaphore()
    for k in range(1, n):
        pl.semaphore_signal(
            barrier, inc=1, device_id={"beam": lax.rem(me + k, n)}, device_id_type=MESH
        )
    has_up = tile > 0
    has_down = tile < tiles - 1

    @pl.when(has_up)
    def _():
        pl.semaphore_signal(barrier, inc=1, device_id={"tile": tile - 1}, device_id_type=MESH)

    @pl.when(has_down)
    def _():
        pl.semaphore_signal(barrier, inc=1, device_id={"tile": tile + 1}, device_id_type=MESH)

    pairs = [
        (scat_in, scat),
        (row_in, row_ref),
        (col_in, col_ref),
        (index_in, index_ref),
        (tilt_in, tilt_ref),
        (coef_in, coef_ref),
        (trig_in, trig_ref),
        (pot_in, pot),
        (meas.at[me, 0], seen),
        (high_in, high_ref),
        (low_in, low_ref),
    ]
    local = [
        pltpu.make_async_copy(src, dst, local_sem.at[i]) for i, (src, dst) in enumerate(pairs)
    ]
    for copy in local:
        copy.start()

    def weights(p):
        corner = row_ref[p] + tile * rows - MARGIN
        picked = index_ref[p]
        result = []
        for b in range(beams):
            turn = (tilt_ref[0, b] * corner + tilt_ref[1, b] * col_ref[p]) & (patch - 1)
            cos, sin = trig_ref[0, turn], trig_ref[1, turn]
            q_re = coef_ref[picked, b]
            q_im = coef_ref[picked + coef_ref.shape[0] // 2, b]
            result.append((q_re * cos + q_im * sin, q_im * cos - q_re * sin))
        return result

    def iota(shape, axis):
        return lax.broadcasted_iota(jnp.int32, shape, axis)

    def ones(mask):
        return jnp.where(mask, 1.0, 0.0).astype(jnp.bfloat16)

    def pick_cols(p):
        shape = (cols, patch)
        return ones(iota(shape, 0) - iota(shape, 1) == col_ref[p])

    def turn_of(p, shape):
        return jnp.where(jnp.full(shape, row_ref[p], jnp.int32) < MARGIN, MARGIN, 0)

    def pick_rows(p):
        shape = (patch, rows)
        wanted = (iota(shape, 0) + turn_of(p, shape)) & (patch - 1)
        return ones(iota(shape, 1) - wanted == row_ref[p] - MARGIN)

    def pick_halo(p, first_row):
        shape = (patch - first_row, 2 * MARGIN)
        held = iota(shape, 1)
        held = jnp.where(held < MARGIN, held, held + rows)
        wanted = (iota(shape, 0) + first_row + turn_of(p, shape)) & (patch - 1)
        return ones(held - wanted == row_ref[p])

    def unturn(value, p):
        turned = jnp.concatenate([value[early:], value[:early]], 0)
        return jnp.where(turn_of(p, value.shape) > 0, turned, value)

    def combine(source, count, coefs):
        total_re = total_im = None
        for b in range(beams):
            re = source[b, 0, :count, :]
            im = source[b, 1, :count, :]
            c_re, c_im = coefs[b]
            now_re = c_re * re - c_im * im
            now_im = c_re * im + c_im * re
            total_re = now_re if total_re is None else total_re + now_re
            total_im = now_im if total_im is None else total_im + now_im
        return jnp.concatenate(split(total_re) + split(total_im), 0)

    def block_of(combined, col_pick, row_pick):
        count = combined.shape[0] // 4
        chosen = dot(combined, col_pick).astype(jnp.bfloat16)
        chosen = jnp.concatenate([chosen[: 2 * count], chosen[2 * count :]], 1)
        return dot(jnp.concatenate([row_pick, row_pick], 1), chosen)

    order = sorted(range(1, n), key=lambda k: abs(2 * k - n))
    coefs = {}
    col_picks = {}

    def make_block(k):
        p = lax.rem(me + k, n)
        coefs[k] = weights(p)
        col_picks[k] = pick_cols(p)
        got = block_of(combine(scat, rows, coefs[k]), col_picks[k], pick_rows(p))
        block[k, 0] = got[:, :patch]
        block[k, 1] = got[:, patch:]

    for copy in local[:7]:
        copy.wait()
    make_block(order[0])

    pl.semaphore_wait(barrier, n - 1 + has_up.astype(jnp.int32) + has_down.astype(jnp.int32))

    def remote(src, dst, send_sem, recv_sem, where):
        return pltpu.make_async_remote_copy(
            src_ref=src,
            dst_ref=dst,
            send_sem=send_sem,
            recv_sem=recv_sem,
            device_id=where,
            device_id_type=MESH,
        )

    last = pl.ds(rows - MARGIN, MARGIN)
    first = pl.ds(0, MARGIN)
    second = pl.ds(MARGIN, MARGIN)
    below = pl.ds(rows + MARGIN, MARGIN)
    up = [
        remote(scat_in.at[:, :, first, :], halo.at[:, :, second, :], halo_send.at[0], halo_recv.at[0], {"tile": tile - 1}),
        remote(pot_in.at[first, :], phalo.at[second, :], halo_send.at[1], halo_recv.at[1], {"tile": tile - 1}),
    ]
    down = [
        remote(scat_in.at[:, :, last, :], halo.at[:, :, first, :], halo_send.at[2], halo_recv.at[2], {"tile": tile + 1}),
        remote(pot_in.at[last, :], phalo.at[first, :], halo_send.at[3], halo_recv.at[3], {"tile": tile + 1}),
    ]

    @pl.when(has_up)
    def _():
        for copy in up:
            copy.start()

    @pl.when(has_down)
    def _():
        for copy in down:
            copy.start()

    @pl.when(tile == 0)
    def _():
        halo[:, :, :MARGIN, :] = jnp.zeros((beams, 2, MARGIN, cols), jnp.float32)
        phalo[:MARGIN, :] = jnp.zeros((MARGIN, cols), jnp.float32)

    @pl.when(tile == tiles - 1)
    def _():
        halo[:, :, MARGIN:, :] = jnp.zeros((beams, 2, MARGIN, cols), jnp.float32)
        phalo[MARGIN:, :] = jnp.zeros((MARGIN, cols), jnp.float32)

    copies_a, copies_b = {}, {}
    for k in order + [0]:
        if k != order[0]:
            make_block(k)
        p = lax.rem(me + k, n)
        if k != 0:
            copies_a[k] = remote(
                block.at[k, :, pl.ds(0, early), :],
                recv_a.at[k - 1],
                a_send.at[k - 1],
                a_recv.at[k - 1],
                {"beam": p},
            )
            copies_a[k].start()


    @pl.when(has_down)
    def _():
        for copy in up:
            copy.wait_recv()

    @pl.when(has_up)
    def _():
        for copy in down:
            copy.wait_recv()

    jobs = [(combine(halo, 2 * MARGIN, coefs[k]), pick_halo(lax.rem(me + k, n), early)) for k in order + [0]]
    for k, (combined, row_pick) in zip(order + [0], jobs):
        p = lax.rem(me + k, n)
        got = block_of(combined, col_picks[k], row_pick)
        for c in range(2):
            send_b[k, c] = block[k, c, early:, :] + got[:, c * patch : (c + 1) * patch]
        if k != 0:
            copies_b[k] = remote(
                send_b.at[k], recv_b.at[k - 1], b_send.at[k - 1], b_recv.at[k - 1], {"beam": p}
            )
            copies_b[k].start()

    local[7].wait()
    tall = jnp.concatenate([pot[...], phalo[...]], 0)
    high, low = split(tall)
    least = (tall - high.astype(jnp.float32) - low.astype(jnp.float32)).astype(jnp.bfloat16)
    row_pick = jnp.concatenate([pick_rows(me), pick_halo(me, 0)], 1)
    here = None
    for term in (least, low, high):
        now = dot(row_pick, dot(term, col_picks[0]).astype(jnp.bfloat16))
        here = now if here is None else here + now
    here = unturn(here, me) * SIGMA_SCALE
    trans[0] = jnp.cos(here)
    trans[1] = jnp.sin(here)

    for k in order:
        copies_a[k].wait_recv()
        copies_b[k].wait_recv()
    for copy in local[8:]:
        copy.wait()

    parts = []
    for c in range(2):
        body = block[0, c, :early, :]
        rest = send_b[0, c]
        for k in order:
            body += recv_a[k - 1, c]
            rest += recv_b[k - 1, c]
        parts.append(unturn(jnp.concatenate([body, rest], 0), me))
    wave_re, wave_im = parts
    exit_re = trans[0] * wave_re - trans[1] * wave_im
    exit_im = trans[0] * wave_im + trans[1] * wave_re
    ahead = (high_ref[0], low_ref[0])
    back = (high_ref[1], low_ref[1])
    far = transform(jnp.concatenate([exit_re, exit_im], 0), back, ahead)
    far_re, far_im = far[:, :patch], far[:, patch:]
    misfit = far_re * far_re + far_im * far_im - seen[...]
    misfit_ref[...] = misfit
    turned = transform(jnp.concatenate([misfit * far_re, misfit * far_im], 0), ahead, back)
    piece[...] = SIGMA_SCALE * (exit_re * turned[:, patch:] - exit_im * turned[:, :patch])

    copies_p = {}
    for k in order:
        copies_p[k] = remote(
            piece, recv_p.at[k - 1], p_send.at[k - 1], p_recv.at[k - 1], {"beam": lax.rem(me + k, n)}
        )
        copies_p[k].start()

    def spots(p):
        shape = (patch, cols)
        col_place = ones(iota(shape, 1) - iota(shape, 0) == col_ref[p])
        shape = (rows + 2 * MARGIN, patch)
        row_place = ones(iota(shape, 0) - iota(shape, 1) == row_ref[p])
        return col_place, jnp.concatenate([row_place, row_place], 1)

    def move(value, spot):
        return dot(jnp.concatenate(split(value), 0), spot[0]).astype(jnp.bfloat16)

    places = [spots(lax.rem(me + n - k, n)) for k in range(n)]
    strip[...] = dot(places[0][1], move(piece[...], places[0]))
    near, far_k = order[1:], order[0]
    for k in near:
        copies_p[k].wait_recv()
    moved = jnp.concatenate([move(recv_p[k - 1], places[k]) for k in near], 0)
    strip[...] += dot(jnp.concatenate([places[k][1] for k in near], 1), moved)
    copies_p[far_k].wait_recv()
    moved = move(recv_p[far_k - 1], places[far_k])
    final_rows = places[far_k][1]
    lower = rows + MARGIN
    rim_rows = jnp.concatenate([final_rows[:MARGIN], final_rows[lower:]], 0)
    rim = dot(rim_rows, moved)
    strip[:MARGIN, :] += rim[:MARGIN]
    strip[lower:, :] += rim[MARGIN:]

    rim_up = remote(strip.at[first, :], rims.at[1], rim_send.at[0], rim_recv.at[0], {"tile": tile - 1})
    rim_down = remote(strip.at[below, :], rims.at[0], rim_send.at[1], rim_recv.at[1], {"tile": tile + 1})

    @pl.when(has_up)
    def _():
        rim_up.start()

    @pl.when(has_down)
    def _():
        rim_down.start()

    grad_ref[...] = strip[MARGIN:lower, :] + dot(final_rows[MARGIN:lower], moved)

    @pl.when(has_down)
    def _():
        rim_up.wait_recv()
        grad_ref[rows - MARGIN :, :] += rims[1]

    @pl.when(has_up)
    def _():
        rim_down.wait_recv()
        grad_ref[:MARGIN, :] += rims[0]

    for k in order:
        copies_a[k].wait_send()
        copies_b[k].wait_send()
        copies_p[k].wait_send()

    @pl.when(has_up)
    def _():
        for copy in up + [rim_up]:
            copy.wait_send()

    @pl.when(has_down)
    def _():
        for copy in down + [rim_down]:
            copy.wait_send()


def hand_over(misfit_in, grad_in, misfit_out, grad_out, misfit, grad, sem):
    pairs = [(misfit_in, misfit, misfit_out), (grad_in, grad, grad_out)]
    ins = [pltpu.make_async_copy(a, b, sem.at[0, i]) for i, (a, b, _) in enumerate(pairs)]
    outs = [pltpu.make_async_copy(b, c, sem.at[1, i]) for i, (_, b, c) in enumerate(pairs)]
    for copy in ins:
        copy.start()
    for here, there in zip(ins, outs):
        here.wait()
        there.start()
    for copy in outs:
        copy.wait()


def shards(
    n,
    tiles,
    scattering,
    potential,
    row_offset,
    col_offset,
    table_index,
    beam_tilt,
    coef_table,
    measured,
):
    beams, _, rows, cols = scattering.shape
    positions, patch = measured.shape[0], measured.shape[-1]
    assert positions == n and patch & (patch - 1) == 0 and cols & (cols - 1) == 0
    high, low, trig = tables(patch)
    coefs = coef_table.reshape(-1, beams)
    f32 = jnp.float32
    early = patch - MARGIN
    i32 = jnp.int32
    vmem = pl.BlockSpec(memory_space=pltpu.VMEM)
    anywhere = pl.BlockSpec(memory_space=pl.ANY)
    strip_rows = rows + 2 * MARGIN
    dma = pltpu.SemaphoreType.DMA
    misfit, grad = pl.pallas_call(
        functools.partial(kernel, n, tiles),
        out_shape=(
            jax.ShapeDtypeStruct((patch, patch), f32),
            jax.ShapeDtypeStruct((rows, cols), f32),
        ),
        in_specs=[anywhere] * 11,
        out_specs=(vmem, vmem),
        scratch_shapes=[
            pltpu.SMEM((n,), i32),
            pltpu.SMEM((n,), i32),
            pltpu.SMEM((n,), i32),
            pltpu.SMEM((2, beams), i32),
            pltpu.SMEM(coefs.shape, f32),
            pltpu.SMEM(trig.shape, f32),
            pltpu.VMEM(high.shape, jnp.bfloat16),
            pltpu.VMEM(low.shape, jnp.bfloat16),
            pltpu.VMEM((beams, 2, rows, cols), f32),
            pltpu.VMEM((rows, cols), f32),
            pltpu.VMEM((beams, 2, 2 * MARGIN, cols), f32),
            pltpu.VMEM((2 * MARGIN, cols), f32),
            pltpu.VMEM((patch, patch), f32),
            pltpu.VMEM((n, 2, patch, patch), f32),
            pltpu.VMEM((n, 2, MARGIN, patch), f32),
            pltpu.VMEM((n - 1, 2, patch - MARGIN, patch), f32),
            pltpu.VMEM((n - 1, 2, MARGIN, patch), f32),
            pltpu.VMEM((2, patch, patch), f32),
            pltpu.VMEM((patch, patch), f32),
            pltpu.VMEM((n - 1, patch, patch), f32),
            pltpu.VMEM((strip_rows, cols), f32),
            pltpu.VMEM((2, MARGIN, cols), f32),
            dma((11,)),
            dma((4,)),
            dma((4,)),
            dma((n - 1,)),
            dma((n - 1,)),
            dma((n - 1,)),
            dma((n - 1,)),
            dma((n - 1,)),
            dma((n - 1,)),
            dma((2,)),
            dma((2,)),
        ],
        compiler_params=pltpu.CompilerParams(
            collective_id=0, has_side_effects=True, vmem_limit_bytes=56 * 1024 * 1024
        ),
    )(
        row_offset[:, 0],
        col_offset[:, 0],
        table_index[:, 0],
        beam_tilt,
        coefs,
        trig,
        high,
        low,
        scattering,
        potential,
        measured,
    )
    shapes = (jax.ShapeDtypeStruct((patch, patch), f32), jax.ShapeDtypeStruct((rows, cols), f32))
    misfit, grad = pl.pallas_call(
        hand_over,
        out_shape=shapes,
        in_specs=[anywhere] * 2,
        out_specs=(anywhere, anywhere),
        scratch_shapes=[pltpu.VMEM(shape.shape, f32) for shape in shapes] + [dma((2, 2))],
        compiler_params=pltpu.CompilerParams(vmem_limit_bytes=56 * 1024 * 1024),
    )(misfit, grad)
    return misfit[None, None], grad


def solution(mesh):
    in_specs = (
        P("beam", None, "tile", None),
        P("tile", None),
        P(None, "tile"),
        P(None, "tile"),
        P(None, "tile"),
        P(None, "beam"),
        P(None, None, "beam"),
        P(None, "tile", None, None),
    )
    out_specs = (P("beam", "tile", None, None), P("tile", None))
    run = functools.partial(shards, mesh.shape["beam"], mesh.shape["tile"])
    return jax.shard_map(run, mesh=mesh, in_specs=in_specs, out_specs=out_specs, check_vma=False)
```
